512 devices in a mesh: grp: 8 (over z), seq: 64 (over y, x, core).
Axes of the slice: x: 4, y: 8, z: 8, core: 2. Of those that a mesh axis runs over, the one named last changes fastest.
Arguments:
- kv_states: bfloat16 [8192, 4096], P('seq'), may hold values from -1.5 to 1.5
- queries_t: bfloat16 [2048, 4096], P('seq', 'grp'), may hold values from -6 to 6
- grad_out_t: bfloat16 [2048, 4096], P('seq', 'grp'), may hold values from -48 to 48
- log_norm: float32 [32, 4096], P(None, 'grp'), may hold values from 1.5 to 2.5
- delta: float32 [32, 4096], P(None, 'grp'), may hold values from -48 to 48
- lengths: int32 [16], P('grp'), may hold values from 1 to 256, 3072 in all
Outputs:
- grad_query_t: bfloat16 [2048, 4096], P('seq', 'grp')
- grad_keys: bfloat16 [8192, 2048], P('seq', 'grp')
- grad_values: bfloat16 [8192, 2048], P('seq', 'grp')
The draws below stay inside these ranges and needn't reach their ends.
Inputs may be any that keep to these rules, and one draw needn't show every extreme that they name: `lengths`: each answer's count of real tokens; one answer is full.
All inputs are finite; a program needn't handle non-finite values. No bound on the sum of `lengths` on one device may be relied on, other than what follows from the above.
Results may differ from the reference program's by a relative error of at most 0.0049.
Values may be sent and summed in bfloat16 or wider, within the bound.
A program may use at most 64 MiB of HBM per device.

```python
import math
import jax
import jax.numpy as jnp
import numpy as np
from jax import lax

HEADS = 32
DH = 64
LEN = 256
TOKENS = 4096
ANSWERS = 16
KEYS = 8192


def level_of(stream_key, dims, cuts, smallest, top_value):
    factor_of = 1.0
    for axis_at, parts in cuts:
        steps = jax.random.uniform(jax.random.fold_in(jax.random.fold_in(stream_key, 6), axis_at), (parts,), jnp.float32, smallest / len(cuts), top_value / len(cuts))
        factor_of = factor_of * jnp.repeat(jnp.exp(steps), dims[axis_at] // parts).reshape((-1,) + (1,) * (len(dims) - 1 - axis_at))
    return factor_of


def length_profile(amount, total, bound, lean):
    portions = [(1 << 20) // math.isqrt(rank ** lean) + 1 for rank in range(2, amount + 1)]
    rest, holding = total - bound - (amount - 1), [1] * (amount - 1)
    while rest > 0:
        candidates = [i for i in range(amount - 1) if holding[i] < bound]
        whole, left = sum([portions[i] for i in candidates]), rest
        for i in candidates:
            addition = min(bound - holding[i], max(1, left * portions[i] // whole), rest)
            holding[i] = holding[i] + addition
            rest = rest - addition
    return np.array([bound] + holding)


def uneven(rng, number_of, total, bound, lean):
    if number_of == 2:
        one = jax.random.randint(rng, (), max(1, total - bound), min(bound, total - 1) + 1)
        return jnp.stack([one, total - one])
    sizes = jnp.asarray(length_profile(number_of, total, bound, lean), jnp.int32)
    couples = (number_of - 1) // 2
    source_of, receiver = sizes[1:1 + 2 * couples:2], sizes[2:2 + 2 * couples:2]
    margin = jnp.minimum(source_of - 1, bound - receiver)
    shifted = jax.random.randint(jax.random.fold_in(rng, 1), (couples,), 0, 1 << 20) % (margin + 1)
    sizes = sizes.at[1:1 + 2 * couples:2].set(source_of - shifted).at[2:2 + 2 * couples:2].set(receiver + shifted)
    return sizes[jax.random.permutation(jax.random.fold_in(rng, 2), number_of)]


def centred(rng, extent, deviation, most, cuts=(), held_as=jnp.bfloat16):
    values = deviation * jax.random.normal(rng, extent, jnp.float32)
    if cuts:
        values = values * level_of(rng, extent, cuts, -0.22, 0.18)
    return jnp.clip(values, -most, most).astype(held_as)


def setup_inputs(seed: int = 0) -> dict:
    arg_keys = jax.random.split(jax.random.key(seed), 7)
    return {
        "kv_states": centred(arg_keys[0], (KEYS, 2 * DH * HEADS), 0.25, 1.5, ((0, 64),)),
        "queries_t": centred(arg_keys[1], (HEADS * DH, TOKENS), 1.0, 6.0, ((0, 64), (1, 8))),
        "grad_out_t": centred(arg_keys[2], (HEADS * DH, TOKENS), 8.0, 48.0, ((0, 64), (1, 8))),
        "log_norm": jnp.clip(1.5 + 1.0 * jax.random.uniform(arg_keys[3], (HEADS, TOKENS), jnp.float32) ** level_of(arg_keys[3], (HEADS, TOKENS), ((1, 8),), -0.2, 0.2), 1.5, 2.5),
        "delta": centred(arg_keys[4], (HEADS, TOKENS), 8.0, 48.0, ((1, 8),), jnp.float32),
        "lengths": uneven(arg_keys[5], ANSWERS, ANSWERS * LEN * 3 // 4, LEN, 2).astype(jnp.int32),
    }


def reference(kv_states, queries_t, grad_out_t, log_norm, delta, lengths):
    width = 2 * DH
    kv_three = kv_states.reshape(KEYS, width, HEADS)
    place = jnp.arange(TOKENS)
    owner = place // LEN
    offset = place % LEN
    valid = offset < lengths[owner]
    block = math.gcd(KEYS, 1024)
    count = KEYS // block

    def per_head(head):
        query = lax.dynamic_slice_in_dim(queries_t, head * DH, DH, 0)
        grad = lax.dynamic_slice_in_dim(grad_out_t, head * DH, DH, 0)
        kv_head = lax.dynamic_index_in_dim(kv_three, head, 2, keepdims=False)
        norm_row = lax.dynamic_index_in_dim(log_norm, head, 0, keepdims=False)
        delta_row = lax.dynamic_index_in_dim(delta, head, 0, keepdims=False)
        pieces = kv_head.reshape(count, block, width)

        def step(carry, piece):
            keys_b = piece[:, :DH]
            vals_b = piece[:, DH:]
            scores = jnp.dot(keys_b, query, preferred_element_type=jnp.float32)
            probs = jnp.where(valid[None, :], jnp.exp(scores - norm_row[None, :]), 0.0) / KEYS
            dprobs = jnp.dot(vals_b, grad, preferred_element_type=jnp.float32)
            dscores = probs * (dprobs - delta_row[None, :])
            probs_b = probs.astype(jnp.bfloat16)
            dscores_b = dscores.astype(jnp.bfloat16)
            dvals = jnp.dot(probs_b, grad.T, preferred_element_type=jnp.float32)
            dkeys = jnp.dot(dscores_b, query.T, preferred_element_type=jnp.float32)
            carry = carry + jnp.dot(keys_b.T, dscores_b, preferred_element_type=jnp.float32)
            return carry, jnp.concatenate([dkeys, dvals], axis=1)

        start = jnp.zeros((DH, TOKENS), jnp.float32)
        dquery, grads = lax.scan(step, start, pieces)
        return dquery, grads.reshape(KEYS, width)

    dqueries, grad_heads = lax.map(per_head, jnp.arange(HEADS))
    grad_query_t = dqueries.reshape(HEADS * DH, TOKENS).astype(jnp.bfloat16)
    key_heads = grad_heads[:, :, :DH]
    value_heads = grad_heads[:, :, DH:]
    grad_keys = jnp.transpose(key_heads, (1, 2, 0)).reshape(KEYS, DH * HEADS).astype(jnp.bfloat16)
    grad_values = jnp.transpose(value_heads, (1, 2, 0)).reshape(KEYS, DH * HEADS).astype(jnp.bfloat16)
    return grad_query_t, grad_keys, grad_values
```

```python
import functools
import math

import jax
import jax.numpy as jnp
from jax import lax
from jax.experimental import pallas as pl
from jax.experimental.pallas import tpu as pltpu
from jax.sharding import PartitionSpec as P

DH = 64
LEN = 256
HALF = DH // 2
STATS = 16
PART = 2 * HALF + STATS
LANES = 128
MESH = pl.DeviceIdType.MESH
F32 = jnp.float32
BF16 = jnp.bfloat16

NT = (((1,), (1,)), ((), ()))
NN = (((1,), (0,)), ((), ()))


def dot(a, b, dims=NN):
    return lax.dot_general(a, b, dims, preferred_element_type=F32)


def exchange_lanes(tiles, unit):
    count = len(tiles)
    lane = lax.broadcasted_iota(jnp.int32, tiles[0].shape, 1)
    step = 1
    while step < count:
        shift = step * unit
        low = (lane & shift) == 0
        made = list(tiles)
        for a in range(count):
            if a & step == 0:
                x, y = tiles[a], tiles[a | step]
                made[a] = jnp.where(low, x, pltpu.roll(y, shift, 1))
                made[a | step] = jnp.where(low, pltpu.roll(x, LANES - shift, 1), y)
        tiles = made
        step *= 2
    return tiles


def kernel(
    n_z, n_h, keys_all,
    kv_hbm, q_hbm, g_hbm, ln_hbm, dl_hbm, len_ref,
    oq_ref, ok_ref, ov_ref,
    kvx, lnv, dlv, kvs, kvb, blocks, lhs, keys_t, acc,
    own_half, sent_half, got_half, dq_out, dq_in, z_out, z_in, p_out, p_in, wide,
    in_sem, kv_send, kv_recv, ring_send, ring_recv, pair_send, pair_recv,
    half_send, half_recv, dq_send, dq_recv, z_send, z_recv, p_send, p_recv,
):
    z = lax.axis_index("grp")
    s = lax.axis_index("seq")
    h = s // 2
    c = s - 2 * h
    partner = 2 * h + 1 - c
    kb = kvx.shape[0]
    tokens = blocks.shape[3]
    span = tokens // 2
    keys = n_h * kb
    last = n_z // 2
    dr = DH // n_z

    loads = [
        pltpu.make_async_copy(kv_hbm.at[pl.ds(pl.multiple_of(z * kb, kb), kb)], kvx, in_sem.at[0]),
        pltpu.make_async_copy(ln_hbm, lnv, in_sem.at[1]),
        pltpu.make_async_copy(dl_hbm, dlv, in_sem.at[2]),
        pltpu.make_async_copy(q_hbm, blocks.at[z, c, pl.ds(0, HALF)], in_sem.at[3]),
        pltpu.make_async_copy(g_hbm, blocks.at[z, c, pl.ds(HALF, HALF)], in_sem.at[4]),
    ]
    for load in loads:
        load.start()

    barrier = pltpu.get_barrier_semaphore()

    def greet_plane(i, _):
        to = lax.rem(h + i, n_h)
        pl.semaphore_signal(barrier, inc=1, device_id=(z, 2 * to + c), device_id_type=MESH)
        return 0

    def greet_line(i, _):
        pl.semaphore_signal(barrier, inc=1, device_id=(lax.rem(z + i, n_z), s), device_id_type=MESH)
        return 0

    lax.fori_loop(1, n_z, greet_line, 0)
    pl.semaphore_signal(barrier, inc=1, device_id=(z, partner), device_id_type=MESH)
    lax.fori_loop(1, n_h, greet_plane, 0)

    loads[1].wait()
    loads[2].wait()
    place = lax.broadcasted_iota(jnp.int32, (1, tokens), 1)
    limit = jnp.zeros((1, tokens), jnp.int32)
    for a in range(tokens // LEN):
        limit = jnp.where(place // LEN == a, len_ref[a], limit)
    norm = -(lnv[pl.ds(h, 1), :] + math.log(keys_all))
    norm = jnp.where(lax.rem(place, LEN) < limit, norm, -1e30)
    row = jnp.where(c == 0, norm, -dlv[pl.ds(h, 1), :])
    high = row.astype(BF16).astype(F32)
    middle = (row - high).astype(BF16).astype(F32)
    low = row - high - middle
    at = lax.broadcasted_iota(jnp.int32, (STATS, tokens), 0)
    rows = jnp.where(at == 0, high, jnp.where(at == 1, middle, jnp.where(at == 2, low, 0.0)))
    blocks[z, c, pl.ds(2 * HALF, STATS)] = rows.astype(BF16)
    loads[3].wait()
    loads[4].wait()

    loads[0].wait()
    tiles = [kvx[:, j * LANES : (j + 1) * LANES].astype(F32) for j in range(n_h)]
    tiles = exchange_lanes(tiles, 1)
    for j in range(n_h):
        kvs[j] = tiles[j].astype(BF16)
    kvb[pl.ds(h, 1)] = kvs[pl.ds(h, 1)]

    pl.semaphore_wait(barrier, n_h - 1 + n_z)

    def ring(way, t, block, columns):
        to = lax.rem(z + (1 if way == 0 else n_z - 1), n_z)
        ref = blocks.at[block, c, :, columns]
        return pltpu.make_async_remote_copy(
            src_ref=ref, dst_ref=ref,
            send_sem=ring_send.at[way, t], recv_sem=ring_recv.at[way, t],
            device_id=(to, s), device_id_type=MESH,
        )

    def pair(i, block):
        ref = blocks.at[block, c]
        return pltpu.make_async_remote_copy(
            src_ref=ref, dst_ref=ref,
            send_sem=pair_send.at[i], recv_sem=pair_recv.at[i],
            device_id=(z, partner), device_id_type=MESH,
        )

    every = pl.ds(0, tokens)
    halves = (pl.ds(0, span), pl.ds(span, span))

    def order(i):
        t = (i + 1) // 2
        return lax.rem(jnp.where(lax.rem(i, 2) == 1, z - t, z + t) + n_z, n_z)

    for way in (0, 1):
        ring(way, 1, z, every if last > 1 else halves[way]).start()
    pair(0, z).start()

    def send_kv(i, _):
        to = lax.rem(h + i, n_h)
        pltpu.make_async_remote_copy(
            src_ref=kvs.at[to], dst_ref=kvb.at[h], send_sem=kv_send, recv_sem=kv_recv,
            device_id=(z, 2 * to + c), device_id_type=MESH,
        ).start()
        return 0

    lax.fori_loop(1, n_h, send_kv, 0)

    def arrive(t):
        @pl.when(t < last)
        def _():
            for way in (0, 1):
                block = order(2 * t - 1 + way)
                ring(way, t, block, every).wait_recv()

                @pl.when(t + 1 < last)
                def _():
                    ring(way, t + 1, block, every).start()

                @pl.when(t + 1 == last)
                def _():
                    ring(way, t + 1, block, halves[way]).start()

                pair(2 * t - 1 + way, block).start()

        @pl.when(t == last)
        def _():
            block = order(n_z - 1)
            for way in (0, 1):
                ring(way, last, block, halves[way]).wait_recv()
            pair(n_z - 1, block).start()

    arrive(jnp.int32(1))

    lane = lax.broadcasted_iota(jnp.int32, (LANES, 2 * PART), 0)
    channel = lax.rem(lane, n_h) * (LANES // n_h) + lane // n_h
    col = lax.broadcasted_iota(jnp.int32, (LANES, 2 * PART), 1)
    side = col // PART
    within = col - side * PART
    is_key = within < HALF
    is_value = (within >= HALF) & (within < 2 * HALF)
    for_scores = jnp.where(is_key & (channel == side * HALF + within), 1.0, 0.0).astype(BF16)
    for_dprobs = jnp.where(
        is_value & (channel == DH + side * HALF + within - HALF), 1.0, 0.0
    ).astype(BF16)
    one = lax.broadcasted_iota(jnp.int32, (keys, 2 * PART), 1)
    ones_s = jnp.where((one >= 2 * HALF) & (one < 2 * HALF + 3), 1.0, 0.0)
    ones_p = jnp.where((one >= PART + 2 * HALF) & (one < PART + 2 * HALF + 3), 1.0, 0.0)
    lane_t = lax.broadcasted_iota(jnp.int32, (DH, LANES), 1)
    channel_t = lax.rem(lane_t, n_h) * (LANES // n_h) + lane_t // n_h
    row_t = lax.broadcasted_iota(jnp.int32, (DH, LANES), 0)
    for_keys = jnp.where(channel_t == row_t, 1.0, 0.0).astype(BF16)

    pltpu.make_async_copy(kvb.at[pl.ds(0, n_h - 1)], kvb.at[pl.ds(0, n_h - 1)], kv_recv).wait()
    mixed = kvb[...].reshape(keys, LANES)
    lhs[0] = (dot(mixed, for_scores) + ones_s).astype(BF16)
    lhs[1] = (dot(mixed, for_dprobs) + ones_p).astype(BF16)
    keys_t[...] = dot(for_keys, mixed, NT).astype(BF16)
    acc[...] = jnp.zeros_like(acc)

    def swap_half(i):
        return pltpu.make_async_remote_copy(
            src_ref=sent_half.at[i], dst_ref=got_half.at[i],
            send_sem=half_send.at[i], recv_sem=half_recv.at[i],
            device_id=(z, partner), device_id_type=MESH,
        )

    def dq_copy(i):
        return pltpu.make_async_remote_copy(
            src_ref=dq_out.at[i], dst_ref=dq_in.at[i], send_sem=dq_send, recv_sem=dq_recv,
            device_id=(order(i), s), device_id_type=MESH,
        )

    def combine(i):
        swap_half(i).wait_recv()
        total = own_half[i] + got_half[i]
        own_half[i] = total
        dq_out[i] = total.astype(BF16)

        @pl.when(i > 0)
        def _():
            dq_copy(i).start()

    chunk = min(keys, 256)

    def compute(i, _):
        @pl.when((lax.rem(i, 2) == 1) & (i // 2 + 2 <= last))
        def _():
            arrive(i // 2 + 2)

        block = order(i)
        pltpu.make_async_copy(
            blocks.at[block, 1 - c], blocks.at[block, 1 - c], pair_recv.at[i]
        ).wait()
        rhs = blocks[block].reshape(2 * PART, tokens)
        blank = jnp.zeros((DH, tokens), BF16)
        q_rows = jnp.concatenate([rhs[:HALF], rhs[PART : PART + HALF], blank], 0)
        g_rows = jnp.concatenate([blank, rhs[HALF:DH], rhs[PART + HALF : PART + DH]], 0)
        dq = jnp.zeros((DH, tokens), F32)
        for k in range(0, keys, chunk):
            part = slice(k, k + chunk)
            probs = jnp.exp(dot(lhs[0, part], rhs))
            dscores = probs * dot(lhs[1, part], rhs)
            probs = probs.astype(BF16)
            dscores = dscores.astype(BF16)
            acc[part] += dot(dscores, q_rows, NT) + dot(probs, g_rows, NT)
            dq += dot(keys_t[:, part], dscores)
        top, bottom = dq[:HALF], dq[HALF:]
        own_half[i] = jnp.where(c == 0, top, bottom)
        sent_half[i] = jnp.where(c == 0, bottom, top)
        swap_half(i).start()

        @pl.when(i > 0)
        def _():
            combine(i - 1)

        return 0

    lax.fori_loop(0, n_z, compute, 0)

    turned = acc[...].T.reshape(2, n_z, dr, keys)
    for g in range(n_z):
        z_out[g] = jnp.concatenate([turned[0, g], turned[1, g]], 0).astype(BF16)
    z_in[pl.ds(z, 1)] = z_out[pl.ds(z, 1)]

    def send_z(i, _):
        to = lax.rem(z + i, n_z)
        pltpu.make_async_remote_copy(
            src_ref=z_out.at[to], dst_ref=z_in.at[z], send_sem=z_send, recv_sem=z_recv,
            device_id=(to, s), device_id_type=MESH,
        ).start()
        return 0

    lax.fori_loop(1, n_z, send_z, 0)
    combine(n_z - 1)
    pltpu.make_async_copy(z_in.at[pl.ds(0, n_z - 1)], z_in.at[pl.ds(0, n_z - 1)], z_recv).wait()

    for j in range(keys // LANES):
        tiles = [z_in[a, :, j * LANES : (j + 1) * LANES].astype(F32) for a in range(n_z)]
        tiles = exchange_lanes(tiles, kb)
        for a in range(n_z):
            p_out[j * n_z + a] = tiles[a].astype(BF16)
    p_in[pl.ds(h, 1)] = p_out[pl.ds(h, 1)]

    def send_p(i, _):
        to = lax.rem(h + i, n_h)
        pltpu.make_async_remote_copy(
            src_ref=p_out.at[to], dst_ref=p_in.at[h], send_sem=p_send, recv_sem=p_recv,
            device_id=(z, 2 * to + c), device_id_type=MESH,
        ).start()
        return 0

    lax.fori_loop(1, n_h, send_p, 0)

    pltpu.make_async_copy(dq_in.at[pl.ds(1, n_z - 1)], dq_in.at[pl.ds(1, n_z - 1)], dq_recv).wait()
    total = own_half[0]
    for i in range(1, n_z):
        total = total + dq_in[i].astype(F32)
    oq_ref[...] = total.astype(BF16)

    pltpu.make_async_copy(p_in.at[pl.ds(0, n_h - 1)], p_in.at[pl.ds(0, n_h - 1)], p_recv).wait()
    wide[...] = p_in[...].astype(F32).reshape(n_h * 2 * dr, LANES)
    for which, ref in enumerate((ok_ref, ov_ref)):
        rows = [wide[pl.ds(which * dr + d, n_h, stride=2 * dr), :] for d in range(dr)]
        ref[...] = jnp.concatenate(rows, 0).T.astype(BF16)

    for way in (0, 1):
        for t in range(1, last + 1):
            ring(way, t, z, every if t < last else halves[way]).wait_send()
    for i in range(n_z):
        pair(i, z).wait_send()
        swap_half(i).wait_send()
    for buf, n, sem in (
        (kvs, n_h - 1, kv_send),
        (dq_out, n_z - 1, dq_send),
        (z_out, n_z - 1, z_send),
        (p_out, n_h - 1, p_send),
    ):
        pltpu.make_async_copy(buf.at[pl.ds(0, n)], buf.at[pl.ds(0, n)], sem).wait()


def on_device(kv_states, queries_t, grad_out_t, log_norm, delta, lengths):
    n_z, n_s = lax.axis_size("grp"), lax.axis_size("seq")
    n_h = n_s // 2
    rows, cols = kv_states.shape
    tokens = queries_t.shape[1]
    kb = rows // n_z
    keys = n_h * kb
    dr = DH // n_z
    last = n_z // 2
    hbm = pl.BlockSpec(memory_space=pl.ANY)
    vmem = pl.BlockSpec(memory_space=pltpu.VMEM)
    dma = pltpu.SemaphoreType.DMA
    return pl.pallas_call(
        functools.partial(kernel, n_z, n_h, rows * n_s),
        out_shape=(
            jax.ShapeDtypeStruct((HALF, tokens), BF16),
            jax.ShapeDtypeStruct((rows, dr * n_h), BF16),
            jax.ShapeDtypeStruct((rows, dr * n_h), BF16),
        ),
        in_specs=[hbm] * 5 + [pl.BlockSpec(memory_space=pltpu.SMEM)],
        out_specs=(vmem,) * 3,
        scratch_shapes=[
            pltpu.VMEM((kb, cols), BF16),
            pltpu.VMEM((n_h, tokens), F32),
            pltpu.VMEM((n_h, tokens), F32),
            pltpu.VMEM((n_h, kb, LANES), BF16),
            pltpu.VMEM((n_h, kb, LANES), BF16),
            pltpu.VMEM((n_z, 2, PART, tokens), BF16),
            pltpu.VMEM((2, keys, 2 * PART), BF16),
            pltpu.VMEM((DH, keys), BF16),
            pltpu.VMEM((keys, 2 * DH), F32),
            pltpu.VMEM((n_z, HALF, tokens), F32),
            pltpu.VMEM((n_z, HALF, tokens), F32),
            pltpu.VMEM((n_z, HALF, tokens), F32),
            pltpu.VMEM((n_z, HALF, tokens), BF16),
            pltpu.VMEM((n_z, HALF, tokens), BF16),
            pltpu.VMEM((n_z, 2 * dr, keys), BF16),
            pltpu.VMEM((n_z, 2 * dr, keys), BF16),
            pltpu.VMEM((n_h, 2 * dr, LANES), BF16),
            pltpu.VMEM((n_h, 2 * dr, LANES), BF16),
            pltpu.VMEM((n_h * 2 * dr, LANES), F32),
            dma((5,)),
            dma, dma,
            dma((2, last + 1)), dma((2, last + 1)),
            dma((n_z,)), dma((n_z,)),
            dma((n_z,)), dma((n_z,)),
            dma, dma, dma, dma, dma, dma,
        ],
        compiler_params=pltpu.CompilerParams(
            collective_id=0, has_side_effects=True, vmem_limit_bytes=48 * 1024 * 1024
        ),
        cost_estimate=pl.CostEstimate(
            flops=10 * DH * keys * tokens * n_z,
            bytes_accessed=4 * 1024 * 1024,
            transcendentals=keys * tokens * n_z,
        ),
    )(kv_states, queries_t, grad_out_t, log_norm, delta, lengths)


def solution(mesh):
    placed = (
        P("seq", None),
        P("seq", "grp"),
        P("seq", "grp"),
        P(None, "grp"),
        P(None, "grp"),
        P("grp"),
    )
    return jax.shard_map(
        on_device,
        mesh=mesh,
        in_specs=placed,
        out_specs=(P("seq", "grp"), P("seq", "grp"), P("seq", "grp")),
        check_vma=False,
    )
```

```python
import functools
import math

import jax
import jax.numpy as jnp
from jax import lax
from jax.experimental import pallas as pl
from jax.experimental.pallas import tpu as pltpu
from jax.sharding import PartitionSpec as P

DH = 64
LEN = 256
HALF = DH // 2
STATS = 16
PART = 2 * HALF + STATS
LANES = 128
MESH = pl.DeviceIdType.MESH
F32 = jnp.float32
BF16 = jnp.bfloat16

NT = (((1,), (1,)), ((), ()))
NN = (((1,), (0,)), ((), ()))


def dot(a, b, dims=NN):
    return lax.dot_general(a, b, dims, preferred_element_type=F32)


def exchange_lanes(tiles, unit):
    count = len(tiles)
    lane = lax.broadcasted_iota(jnp.int32, tiles[0].shape, 1)
    step = 1
    while step < count:
        shift = step * unit
        low = (lane & shift) == 0
        made = list(tiles)
        for a in range(count):
            if a & step == 0:
                x, y = tiles[a], tiles[a | step]
                made[a] = jnp.where(low, x, pltpu.roll(y, shift, 1))
                made[a | step] = jnp.where(low, pltpu.roll(x, LANES - shift, 1), y)
        tiles = made
        step *= 2
    return tiles


def kernel(
    n_z, n_h, keys_all,
    kv_hbm, q_hbm, g_hbm, ln_hbm, dl_hbm, len_ref,
    oq_ref, ok_ref, ov_ref,
    kvx, lnv, dlv, kvs, kvb, blocks, lhs, keys_t, acc,
    own_half, sent_half, got_half, dq_out, dq_in, p_out, p_in, wide,
    in_sem, kv_send, kv_recv, near_send, near_recv, far_send, far_recv,
    third_send, third_recv, fourth_send, fourth_recv, pair_send, pair_recv,
    half_send, half_recv, dq_send, dq_recv, p_send, p_recv,
):
    z = lax.axis_index("grp")
    s = lax.axis_index("seq")
    h = s // 2
    c = s - 2 * h
    partner = 2 * h + 1 - c
    rows = kvx.shape[0]
    tokens = blocks.shape[3]
    span = tokens // 2
    slots = kvb.shape[0]
    keys = slots * rows
    dr = DH // n_z

    width = n_z // 2
    run = h // width
    is_source = (lax.rem(h - run + n_h * width, width) == z // 2) & (c == lax.rem(z, 2))
    serves = lax.rem(run, 2)

    def source(slot):
        at = 2 * slot + c
        return 2 * (at * width + lax.rem(z // 2 + at, width)) + lax.rem(z, 2)

    own_slot = run // 2
    to_self = is_source & (serves == c)

    barrier = pltpu.get_barrier_semaphore()

    def greet(device):
        pl.semaphore_signal(barrier, inc=1, device_id=device, device_id_type=MESH)

    def greet_source(i, _):
        @pl.when(source(i) != s)
        def _():
            greet((z, source(i)))

        return 0

    def greet_line(i, _):
        greet((lax.rem(z + i, n_z), s))
        return 0

    lax.fori_loop(0, slots, greet_source, 0)
    lax.fori_loop(1, n_z, greet_line, 0)
    greet((z, partner))

    loads = [
        pltpu.make_async_copy(ln_hbm, lnv, in_sem.at[0]),
        pltpu.make_async_copy(dl_hbm, dlv, in_sem.at[1]),
        pltpu.make_async_copy(q_hbm, blocks.at[z, c, pl.ds(0, HALF)], in_sem.at[2]),
        pltpu.make_async_copy(g_hbm, blocks.at[z, c, pl.ds(HALF, HALF)], in_sem.at[3]),
    ]
    for load in loads:
        load.start()
    load_kv = pltpu.make_async_copy(kv_hbm, kvx, in_sem.at[4])

    @pl.when(is_source)
    def _():
        load_kv.start()

    loads[0].wait()
    loads[1].wait()
    place = lax.broadcasted_iota(jnp.int32, (1, tokens), 1)
    limit = jnp.zeros((1, tokens), jnp.int32)
    for a in range(tokens // LEN):
        limit = jnp.where(place // LEN == a, len_ref[a], limit)
    norm = -(lnv[pl.ds(h, 1), :] + math.log(keys_all))
    norm = jnp.where(lax.rem(place, LEN) < limit, norm, -1e30)
    row = jnp.where(c == 0, norm, -dlv[pl.ds(h, 1), :])
    high = row.astype(BF16).astype(F32)
    middle = (row - high).astype(BF16).astype(F32)
    low = row - high - middle
    at = lax.broadcasted_iota(jnp.int32, (STATS, tokens), 0)
    parts = jnp.where(at == 0, high, jnp.where(at == 1, middle, jnp.where(at == 2, low, 0.0)))
    blocks[z, c, pl.ds(2 * HALF, STATS)] = parts.astype(BF16)
    loads[2].wait()
    loads[3].wait()

    @pl.when(is_source)
    def _():
        load_kv.wait()

        def sort(r, _):
            part = pl.ds(pl.multiple_of(r * STATS, STATS), STATS)
            tiles = [kvx[part, j * LANES : (j + 1) * LANES].astype(F32) for j in range(n_h)]
            tiles = exchange_lanes(tiles, 1)
            for j in range(n_h):
                kvs[j, part] = tiles[j].astype(BF16)
            return 0

        lax.fori_loop(0, rows // STATS, sort, 0)

        @pl.when(serves == c)
        def _():
            kvb[pl.ds(own_slot, 1)] = kvs[pl.ds(h, 1)]

    served = jnp.where(is_source, n_h - jnp.where(serves == c, 1, 0), 0)
    pl.semaphore_wait(barrier, n_z + served)

    every = pl.ds(0, tokens)
    halves = (pl.ds(0, span), pl.ds(span, span))

    def order(i):
        t = (i + 1) // 2
        return lax.rem(jnp.where(lax.rem(i, 2) == 1, z - t, z + t) + n_z, n_z)

    def along(way, hops, block, columns, send, recv):
        to = lax.rem(z + (hops if way == 0 else n_z - hops), n_z)
        ref = blocks.at[block, c, :, columns]
        return pltpu.make_async_remote_copy(
            src_ref=ref, dst_ref=ref, send_sem=send, recv_sem=recv,
            device_id=(to, s), device_id_type=MESH,
        )

    def near(way):
        return along(way, 1, z, every, near_send.at[way], near_recv.at[way])

    def far(way, half):
        return along(way, 2, z, halves[half], far_send.at[way, half], far_recv.at[way, half])

    def third(way, half):
        block = order(3 + way)
        return along(way, 1, block, halves[half], third_send.at[way, half], third_recv.at[way, half])

    def fourth(way):
        return along(way, 2, order(3 + way), halves[way], fourth_send.at[way], fourth_recv.at[way])

    def pair(i):
        ref = blocks.at[order(i), c]
        return pltpu.make_async_remote_copy(
            src_ref=ref, dst_ref=ref,
            send_sem=pair_send.at[i], recv_sem=pair_recv.at[i],
            device_id=(z, partner), device_id_type=MESH,
        )

    for half in (0, 1):
        for way in (0, 1):
            far(way, half).start()
    for way in (0, 1):
        near(way).start()
    pair(0).start()

    def kv_copy(to):
        return pltpu.make_async_remote_copy(
            src_ref=kvs.at[to], dst_ref=kvb.at[own_slot],
            send_sem=kv_send, recv_sem=kv_recv.at[own_slot],
            device_id=(z, 2 * to + serves), device_id_type=MESH,
        )

    def send_kv(i, _):
        to = lax.rem(h + n_h // 2 + i, n_h)

        @pl.when(2 * to + serves != s)
        def _():
            kv_copy(to).start()

        return 0

    @pl.when(is_source)
    def _():
        lax.fori_loop(0, n_h, send_kv, 0)

    lane = lax.broadcasted_iota(jnp.int32, (LANES, 2 * PART), 0)
    channel = lax.rem(lane, n_h) * (LANES // n_h) + lane // n_h
    col = lax.broadcasted_iota(jnp.int32, (LANES, 2 * PART), 1)
    side = col // PART
    within = col - side * PART
    is_key = within < HALF
    is_value = (within >= HALF) & (within < 2 * HALF)
    for_scores = jnp.where(is_key & (channel == side * HALF + within), 1.0, 0.0).astype(BF16)
    for_dprobs = jnp.where(
        is_value & (channel == DH + side * HALF + within - HALF), 1.0, 0.0
    ).astype(BF16)
    one = lax.broadcasted_iota(jnp.int32, (1, 2 * PART), 1)
    ones_s = jnp.where((one >= 2 * HALF) & (one < 2 * HALF + 3), 1.0, 0.0)
    ones_p = jnp.where((one >= PART + 2 * HALF) & (one < PART + 2 * HALF + 3), 1.0, 0.0)
    lane_t = lax.broadcasted_iota(jnp.int32, (DH, LANES), 1)
    channel_t = lax.rem(lane_t, n_h) * (LANES // n_h) + lane_t // n_h
    row_t = lax.broadcasted_iota(jnp.int32, (DH, LANES), 0)
    for_keys = jnp.where(channel_t == row_t, 1.0, 0.0).astype(BF16)
    acc[...] = jnp.zeros_like(acc)

    for half in (0, 1):
        for way in (0, 1):
            far(way, half).wait_recv()
            third(way, half).start()
            if way == half:
                fourth(way).start()
    for way in (0, 1):
        near(way).wait_recv()
        pair(1 + way).start()
    for way in (0, 1):
        pair(3 + way).start()

    for slot in range(slots):

        @pl.when(jnp.logical_not(to_self & (own_slot == slot)))
        def _():
            pltpu.make_async_copy(kvb.at[slot], kvb.at[slot], kv_recv.at[slot]).wait()

    mixed = kvb[...].reshape(keys, LANES)
    lhs[0] = (dot(mixed, for_scores) + ones_s).astype(BF16)
    lhs[1] = (dot(mixed, for_dprobs) + ones_p).astype(BF16)
    keys_t[...] = dot(for_keys, mixed, NT).astype(BF16)

    def swap_half(i):
        return pltpu.make_async_remote_copy(
            src_ref=sent_half.at[i], dst_ref=got_half.at[i],
            send_sem=half_send.at[i], recv_sem=half_recv.at[i],
            device_id=(z, partner), device_id_type=MESH,
        )

    def dq_copy(i):
        return pltpu.make_async_remote_copy(
            src_ref=dq_out.at[i], dst_ref=dq_in.at[i], send_sem=dq_send, recv_sem=dq_recv,
            device_id=(order(i), s), device_id_type=MESH,
        )

    def combine(i):
        swap_half(i).wait_recv()
        total = own_half[i] + got_half[i]
        own_half[i] = total
        dq_out[i] = total.astype(BF16)

        @pl.when(i > 0)
        def _():
            dq_copy(i).start()

    chunk = min(keys, 256)

    def compute(i, _):
        @pl.when(i == 3)
        def _():
            for way in (0, 1):
                for half in (0, 1):
                    third(way, half).wait_recv()
                pair(5 + way).start()

        @pl.when(i == 5)
        def _():
            for way in (0, 1):
                fourth(way).wait_recv()
            pair(7).start()

        block = order(i)
        pltpu.make_async_copy(
            blocks.at[block, 1 - c], blocks.at[block, 1 - c], pair_recv.at[i]
        ).wait()
        rhs = blocks[block].reshape(2 * PART, tokens)
        blank = jnp.zeros((DH, tokens), BF16)
        q_rows = jnp.concatenate([rhs[:HALF], rhs[PART : PART + HALF], blank], 0)
        g_rows = jnp.concatenate([blank, rhs[HALF:DH], rhs[PART + HALF : PART + DH]], 0)
        dq = jnp.zeros((DH, tokens), F32)
        for k in range(0, keys, chunk):
            part = slice(k, k + chunk)
            probs = jnp.exp(dot(lhs[0, part], rhs))
            dscores = probs * dot(lhs[1, part], rhs)
            probs = probs.astype(BF16)
            dscores = dscores.astype(BF16)
            acc[part] += dot(dscores, q_rows, NT) + dot(probs, g_rows, NT)
            dq += dot(keys_t[:, part], dscores)
        top, bottom = dq[:HALF], dq[HALF:]
        own_half[i] = jnp.where(c == 0, top, bottom)
        sent_half[i] = jnp.where(c == 0, bottom, top)
        swap_half(i).start()

        @pl.when(i > 0)
        def _():
            combine(i - 1)

        return 0

    lax.fori_loop(0, n_z, compute, 0)

    turned = acc[...].T.reshape(2, n_z, dr, keys)
    for slot in range(slots):
        columns = slice(slot * rows, (slot + 1) * rows)
        for g in range(n_z):
            tile = jnp.concatenate([turned[0, g, :, columns], turned[1, g, :, columns]], 0)
            p_out[slot * n_z + g] = tile.astype(BF16)

    @pl.when(to_self)
    def _():
        p_in[pl.ds(h, 1)] = p_out[pl.ds(own_slot * n_z + z, 1)]

    def send_p(i, _):
        slot = lax.rem(i // n_z + h, slots)
        g = lax.rem(z + n_z // 2 + i, n_z)

        @pl.when((g != z) | (source(slot) != s))
        def _():
            pltpu.make_async_remote_copy(
                src_ref=p_out.at[slot * n_z + g], dst_ref=p_in.at[h],
                send_sem=p_send, recv_sem=p_recv,
                device_id=(g, source(slot)), device_id_type=MESH,
            ).start()

        return 0

    lax.fori_loop(0, slots * n_z, send_p, 0)
    combine(n_z - 1)

    pltpu.make_async_copy(dq_in.at[pl.ds(1, n_z - 1)], dq_in.at[pl.ds(1, n_z - 1)], dq_recv).wait()
    total = own_half[0]
    for i in range(1, n_z):
        total = total + dq_in[i].astype(F32)
    oq_ref[...] = total.astype(BF16)

    def settle(buf, n, sem):
        pltpu.make_async_copy(buf.at[pl.ds(0, n)], buf.at[pl.ds(0, n)], sem).wait()

    @pl.when(to_self)
    def _():
        settle(p_in, n_h - 1, p_recv)

    @pl.when(jnp.logical_not(to_self))
    def _():
        settle(p_in, n_h, p_recv)

    wide[...] = p_in[...].astype(F32).reshape(n_h * 2 * dr, LANES)
    for which, ref in enumerate((ok_ref, ov_ref)):
        picked = [wide[pl.ds(which * dr + d, n_h, stride=2 * dr), :] for d in range(dr)]
        ref[...] = jnp.concatenate(picked, 0).T.astype(BF16)

    for way in (0, 1):
        near(way).wait_send()
        fourth(way).wait_send()
        for half in (0, 1):
            far(way, half).wait_send()
            third(way, half).wait_send()
    for i in range(n_z):
        pair(i).wait_send()
        swap_half(i).wait_send()
    settle(dq_out, n_z - 1, dq_send)

    @pl.when(to_self)
    def _():
        settle(p_out, slots * n_z - 1, p_send)
        settle(kvs, n_h - 1, kv_send)

    @pl.when(jnp.logical_not(to_self))
    def _():
        settle(p_out, slots * n_z, p_send)

    @pl.when(is_source & (serves != c))
    def _():
        settle(kvs, n_h, kv_send)


def on_device(kv_states, queries_t, grad_out_t, log_norm, delta, lengths):
    n_z, n_s = lax.axis_size("grp"), lax.axis_size("seq")
    n_h = n_s // 2
    rows, cols = kv_states.shape
    tokens = queries_t.shape[1]
    slots = n_h // n_z
    keys = slots * rows
    dr = DH // n_z
    hbm = pl.BlockSpec(memory_space=pl.ANY)
    vmem = pl.BlockSpec(memory_space=pltpu.VMEM)
    dma = pltpu.SemaphoreType.DMA
    return pl.pallas_call(
        functools.partial(kernel, n_z, n_h, rows * n_s),
        out_shape=(
            jax.ShapeDtypeStruct((HALF, tokens), BF16),
            jax.ShapeDtypeStruct((rows, dr * n_h), BF16),
            jax.ShapeDtypeStruct((rows, dr * n_h), BF16),
        ),
        in_specs=[hbm] * 5 + [pl.BlockSpec(memory_space=pltpu.SMEM)],
        out_specs=(vmem,) * 3,
        scratch_shapes=[
            pltpu.VMEM((rows, cols), BF16),
            pltpu.VMEM((n_h, tokens), F32),
            pltpu.VMEM((n_h, tokens), F32),
            pltpu.VMEM((n_h, rows, LANES), BF16),
            pltpu.VMEM((slots, rows, LANES), BF16),
            pltpu.VMEM((n_z, 2, PART, tokens), BF16),
            pltpu.VMEM((2, keys, 2 * PART), BF16),
            pltpu.VMEM((DH, keys), BF16),
            pltpu.VMEM((keys, 2 * DH), F32),
            pltpu.VMEM((n_z, HALF, tokens), F32),
            pltpu.VMEM((n_z, HALF, tokens), F32),
            pltpu.VMEM((n_z, HALF, tokens), F32),
            pltpu.VMEM((n_z, HALF, tokens), BF16),
            pltpu.VMEM((n_z, HALF, tokens), BF16),
            pltpu.VMEM((slots * n_z, 2 * dr, LANES), BF16),
            pltpu.VMEM((n_h, 2 * dr, LANES), BF16),
            pltpu.VMEM((n_h * 2 * dr, LANES), F32),
            dma((5,)),
            dma, dma((slots,)),
            dma((2,)), dma((2,)),
            dma((2, 2)), dma((2, 2)),
            dma((2, 2)), dma((2, 2)),
            dma((2,)), dma((2,)),
            dma((n_z,)), dma((n_z,)),
            dma((n_z,)), dma((n_z,)),
            dma, dma, dma, dma,
        ],
        compiler_params=pltpu.CompilerParams(
            collective_id=0, has_side_effects=True, vmem_limit_bytes=63 * 1024 * 1024
        ),
        cost_estimate=pl.CostEstimate(
            flops=10 * DH * keys * tokens * n_z,
            bytes_accessed=4 * 1024 * 1024,
            transcendentals=keys * tokens * n_z,
        ),
    )(kv_states, queries_t, grad_out_t, log_norm, delta, lengths)


def solution(mesh):
    placed = (
        P("seq", None),
        P("seq", "grp"),
        P("seq", "grp"),
        P(None, "grp"),
        P(None, "grp"),
        P("grp"),
    )
    return jax.shard_map(
        on_device,
        mesh=mesh,
        in_specs=placed,
        out_specs=(P("seq", "grp"), P("seq", "grp"), P("seq", "grp")),
        check_vma=False,
    )
```

```python
import functools
import math

import jax
import jax.numpy as jnp
from jax import lax
from jax.experimental import pallas as pl
from jax.experimental.pallas import tpu as pltpu
from jax.sharding import PartitionSpec as P

DH = 64
LEN = 256
HALF = DH // 2
STATS = 16
PART = 2 * HALF + STATS
LANES = 128
MESH = pl.DeviceIdType.MESH
F32 = jnp.float32
BF16 = jnp.bfloat16

NT = (((1,), (1,)), ((), ()))
NN = (((1,), (0,)), ((), ()))


def dot(a, b, dims=NN):
    return lax.dot_general(a, b, dims, preferred_element_type=F32)


def exchange_lanes(tiles, unit):
    count = len(tiles)
    lane = lax.broadcasted_iota(jnp.int32, tiles[0].shape, 1)
    step = 1
    while step < count:
        shift = step * unit
        low = (lane & shift) == 0
        made = list(tiles)
        for a in range(count):
            if a & step == 0:
                x, y = tiles[a], tiles[a | step]
                made[a] = jnp.where(low, x, pltpu.roll(y, shift, 1))
                made[a | step] = jnp.where(low, pltpu.roll(x, LANES - shift, 1), y)
        tiles = made
        step *= 2
    return tiles


def kernel(
    n_z, n_h, keys_all,
    kv_hbm, q_hbm, g_hbm, ln_hbm, dl_hbm, len_ref,
    oq_ref, op_ref,
    kvx, lnv, dlv, kvs, kvb, blocks, lhs, keys_t, acc,
    dq_sum, own_half, sent_half, got_half, dq_out, dq_in, p_out, p_in,
    in_sem, kv_send, kv_recv, near_send, near_recv, far_send, far_recv,
    third_send, third_recv, fourth_send, fourth_recv, pair_send, pair_recv,
    half_send, half_recv, dq_send, dq_recv, p_send, p_recv,
):
    z = lax.axis_index("grp")
    s = lax.axis_index("seq")
    h = s // 2
    c = s - 2 * h
    partner = 2 * h + 1 - c
    rows = kvx.shape[0]
    tokens = blocks.shape[3]
    span = tokens // 2
    slots = kvb.shape[0]
    chunk = slots * rows // 2
    dr = DH // n_z

    width = n_z // 2
    runs = n_h // width
    run = h // width
    turn = z // 2
    is_source = c == lax.rem(z, 2)
    to_self = (z == 0) & (c == 0)

    def choose(table, i):
        out = jnp.int32(table[-1])
        for k in range(len(table) - 1):
            out = jnp.where(i == k, table[k], out)
        return out

    def chip_at(away, along_run):
        return lax.rem(run + away, runs) * width + lax.rem(h - run * width + along_run, width)

    def source(place):
        away = jnp.where(c == 0, choose((0, 2, 6, 4), place), choose((1, 7, 3, 5), place))
        return 2 * chip_at(away, turn + away) + lax.rem(z, 2)

    barrier = pltpu.get_barrier_semaphore()

    def greet(device):
        pl.semaphore_signal(barrier, inc=1, device_id=device, device_id_type=MESH)

    def greet_source(i, _):
        @pl.when(jnp.logical_not(to_self & (i == 0)))
        def _():
            greet((z, source(i)))

        return 0

    def greet_line(i, _):
        greet((lax.rem(z + i, n_z), s))
        return 0

    lax.fori_loop(0, slots, greet_source, 0)
    lax.fori_loop(1, n_z, greet_line, 0)
    greet((z, partner))

    loads = [
        pltpu.make_async_copy(ln_hbm, lnv, in_sem.at[0]),
        pltpu.make_async_copy(dl_hbm, dlv, in_sem.at[1]),
        pltpu.make_async_copy(q_hbm, blocks.at[z, c, pl.ds(0, HALF)], in_sem.at[2]),
        pltpu.make_async_copy(g_hbm, blocks.at[z, c, pl.ds(HALF, HALF)], in_sem.at[3]),
    ]
    for load in loads:
        load.start()
    load_kv = pltpu.make_async_copy(kv_hbm, kvx, in_sem.at[4])

    @pl.when(is_source)
    def _():
        load_kv.start()

    loads[0].wait()
    loads[1].wait()
    place = lax.broadcasted_iota(jnp.int32, (1, tokens), 1)
    limit = jnp.zeros((1, tokens), jnp.int32)
    for a in range(tokens // LEN):
        limit = jnp.where(place // LEN == a, len_ref[a], limit)
    norm = -(lnv[pl.ds(h, 1), :] + math.log(keys_all))
    norm = jnp.where(lax.rem(place, LEN) < limit, norm, -1e30)
    row = jnp.where(c == 0, norm, -dlv[pl.ds(h, 1), :])
    high = row.astype(BF16).astype(F32)
    middle = (row - high).astype(BF16).astype(F32)
    low = row - high - middle
    at = lax.broadcasted_iota(jnp.int32, (STATS, tokens), 0)
    parts = jnp.where(at == 0, high, jnp.where(at == 1, middle, jnp.where(at == 2, low, 0.0)))
    blocks[z, c, pl.ds(2 * HALF, STATS)] = parts.astype(BF16)
    loads[2].wait()
    loads[3].wait()

    @pl.when(is_source)
    def _():
        load_kv.wait()

        def sort(r, _):
            part = pl.ds(pl.multiple_of(r * STATS, STATS), STATS)
            tiles = [kvx[part, j * LANES : (j + 1) * LANES].astype(F32) for j in range(n_h)]
            tiles = exchange_lanes(tiles, 1)
            for j in range(n_h):
                kvs[j, part] = tiles[j].astype(BF16)
            return 0

        lax.fori_loop(0, rows // STATS, sort, 0)

        @pl.when(to_self)
        def _():
            kvb[0] = kvs[h]

    served = jnp.where(is_source, runs - jnp.where(to_self, 1, 0), 0)
    pl.semaphore_wait(barrier, n_z + served)

    every = pl.ds(0, tokens)
    halves = (pl.ds(0, span), pl.ds(span, span))

    def order(i):
        t = (i + 1) // 2
        return lax.rem(jnp.where(lax.rem(i, 2) == 1, z - t, z + t) + n_z, n_z)

    def along(way, hops, block, columns, send, recv):
        to = lax.rem(z + (hops if way == 0 else n_z - hops), n_z)
        ref = blocks.at[block, c, :, columns]
        return pltpu.make_async_remote_copy(
            src_ref=ref, dst_ref=ref, send_sem=send, recv_sem=recv,
            device_id=(to, s), device_id_type=MESH,
        )

    def near(way):
        return along(way, 1, z, every, near_send.at[way], near_recv.at[way])

    def far(way, half):
        return along(way, 2, z, halves[half], far_send.at[way, half], far_recv.at[way, half])

    def third(way, half):
        block = order(3 + way)
        return along(way, 1, block, halves[half], third_send.at[way, half], third_recv.at[way, half])

    def fourth(way):
        return along(way, 2, order(3 + way), halves[way], fourth_send.at[way], fourth_recv.at[way])

    def pair(i):
        ref = blocks.at[order(i), c]
        return pltpu.make_async_remote_copy(
            src_ref=ref, dst_ref=ref,
            send_sem=pair_send.at[i], recv_sem=pair_recv.at[i],
            device_id=(z, partner), device_id_type=MESH,
        )

    for half in (0, 1):
        for way in (0, 1):
            far(way, half).start()
    for way in (0, 1):
        near(way).start()
    pair(0).start()

    def send_kv(i, _):
        away = lax.rem(i + runs // 2, runs)
        to = chip_at(runs - away, 2 * runs - turn - away)
        place = choose((0, 0, 1, 2, 3, 3, 2, 1), away)

        @pl.when(jnp.logical_not(to_self & (away == 0)))
        def _():
            pltpu.make_async_remote_copy(
                src_ref=kvs.at[to], dst_ref=kvb.at[place],
                send_sem=kv_send, recv_sem=kv_recv.at[place],
                device_id=(z, 2 * to + lax.rem(away, 2)), device_id_type=MESH,
            ).start()

        return 0

    @pl.when(is_source)
    def _():
        lax.fori_loop(0, runs, send_kv, 0)

    lane = lax.broadcasted_iota(jnp.int32, (LANES, 2 * PART), 0)
    channel = lax.rem(lane, n_h) * (LANES // n_h) + lane // n_h
    col = lax.broadcasted_iota(jnp.int32, (LANES, 2 * PART), 1)
    side = col // PART
    within = col - side * PART
    is_key = within < HALF
    is_value = (within >= HALF) & (within < 2 * HALF)
    for_scores = jnp.where(is_key & (channel == side * HALF + within), 1.0, 0.0).astype(BF16)
    for_dprobs = jnp.where(
        is_value & (channel == DH + side * HALF + within - HALF), 1.0, 0.0
    ).astype(BF16)
    one = lax.broadcasted_iota(jnp.int32, (1, 2 * PART), 1)
    ones_s = jnp.where((one >= 2 * HALF) & (one < 2 * HALF + 3), 1.0, 0.0)
    ones_p = jnp.where((one >= PART + 2 * HALF) & (one < PART + 2 * HALF + 3), 1.0, 0.0)
    lane_t = lax.broadcasted_iota(jnp.int32, (DH, LANES), 1)
    channel_t = lax.rem(lane_t, n_h) * (LANES // n_h) + lane_t // n_h
    row_t = lax.broadcasted_iota(jnp.int32, (DH, LANES), 0)
    for_keys = jnp.where(channel_t == row_t, 1.0, 0.0).astype(BF16)
    acc[...] = jnp.zeros_like(acc)

    for half in (0, 1):
        for way in (0, 1):
            far(way, half).wait_recv()
            third(way, half).start()
            if way == half:
                fourth(way).start()
    for way in (0, 1):
        near(way).wait_recv()
        pair(1 + way).start()
    for way in (0, 1):
        pair(3 + way).start()

    def keys_in(part):
        for place in (part * slots // 2, part * slots // 2 + 1):

            @pl.when(jnp.logical_not(to_self & (place == 0)))
            def _():
                pltpu.make_async_copy(kvb.at[place], kvb.at[place], kv_recv.at[place]).wait()

        at = pl.ds(part * chunk, chunk)
        mixed = kvb[pl.ds(part * slots // 2, slots // 2)].reshape(chunk, LANES)
        lhs[0, at] = (dot(mixed, for_scores) + ones_s).astype(BF16)
        lhs[1, at] = (dot(mixed, for_dprobs) + ones_p).astype(BF16)
        keys_t[part] = dot(for_keys, mixed, NT).astype(BF16)

    keys_in(0)

    def swap_half(i):
        return pltpu.make_async_remote_copy(
            src_ref=sent_half.at[i], dst_ref=got_half.at[i],
            send_sem=half_send.at[i], recv_sem=half_recv.at[i],
            device_id=(z, partner), device_id_type=MESH,
        )

    def dq_copy(i):
        return pltpu.make_async_remote_copy(
            src_ref=dq_out.at[i], dst_ref=dq_in.at[i], send_sem=dq_send, recv_sem=dq_recv,
            device_id=(order(i), s), device_id_type=MESH,
        )

    def combine(i):
        swap_half(i).wait_recv()
        total = own_half[i] + got_half[i]
        own_half[i] = total
        dq_out[i] = total.astype(BF16)

        @pl.when(i > 0)
        def _():
            dq_copy(i).start()

    def send_keys(part):
        turned = acc[part * chunk : (part + 1) * chunk].T.reshape(2, n_z, dr, chunk)
        first = part * slots // 2
        for place in range(slots // 2):
            columns = slice(place * rows, (place + 1) * rows)
            for g in range(n_z):
                tile = jnp.concatenate([turned[0, g, :, columns], turned[1, g, :, columns]], 0)
                p_out[(first + place) * n_z + g] = tile.astype(BF16)
        if part == 0:

            @pl.when(to_self)
            def _():
                p_in[pl.ds(h, 1)] = p_out[pl.ds(z, 1)]

        def send(i, _):
            place = first + i // n_z
            g = lax.rem(z + n_z // 2 + i, n_z)

            @pl.when(jnp.logical_not(to_self & (place == 0) & (g == z)))
            def _():
                pltpu.make_async_remote_copy(
                    src_ref=p_out.at[place * n_z + g], dst_ref=p_in.at[h],
                    send_sem=p_send, recv_sem=p_recv,
                    device_id=(g, source(place)), device_id_type=MESH,
                ).start()

            return 0

        lax.fori_loop(0, slots // 2 * n_z, send, 0)

    table_part = (0, 0, 0, 1, 1, 1, 1, 1, 0, 1, 0, 1, 0, 1, 0, 0)
    table_step = (3, 4, 0, 3, 4, 0, 1, 2, 5, 5, 6, 6, 7, 7, 1, 2)
    table_ends = (0, 0, 0, 1, 1, 1, 0, 0, 0, 1, 0, 1, 0, 1, 1, 1)

    def compute(j, _):
        part = choose(table_part, j)
        i = choose(table_step, j)
        opens = choose(table_ends, j) == 0

        @pl.when(j == 3)
        def _():
            keys_in(1)

        @pl.when(j == 5)
        def _():
            for way in (0, 1):
                for half in (0, 1):
                    third(way, half).wait_recv()
                pair(5 + way).start()

        @pl.when(j == 7)
        def _():
            for way in (0, 1):
                fourth(way).wait_recv()
            pair(7).start()

        @pl.when(j == 14)
        def _():
            send_keys(1)

        block = order(i)

        @pl.when(opens)
        def _():
            pltpu.make_async_copy(
                blocks.at[block, 1 - c], blocks.at[block, 1 - c], pair_recv.at[i]
            ).wait()

        rhs = blocks[block].reshape(2 * PART, tokens)
        blank = jnp.zeros((DH, tokens), BF16)
        q_rows = jnp.concatenate([rhs[:HALF], rhs[PART : PART + HALF], blank], 0)
        g_rows = jnp.concatenate([blank, rhs[HALF:DH], rhs[PART + HALF : PART + DH]], 0)
        at = pl.ds(pl.multiple_of(part * chunk, chunk), chunk)
        probs = jnp.exp(dot(lhs[0, at], rhs))
        dscores = probs * dot(lhs[1, at], rhs)
        probs = probs.astype(BF16)
        dscores = dscores.astype(BF16)
        acc[at] += dot(dscores, q_rows, NT) + dot(probs, g_rows, NT)
        dq = dot(keys_t[part], dscores)

        @pl.when(opens)
        def _():
            dq_sum[i] = dq

        @pl.when(jnp.logical_not(opens))
        def _():
            total = dq_sum[i] + dq
            top, bottom = total[:HALF], total[HALF:]
            own_half[i] = jnp.where(c == 0, top, bottom)
            sent_half[i] = jnp.where(c == 0, bottom, top)
            swap_half(i).start()

        @pl.when((j >= 2) & (choose(table_ends, j - 2) == 1))
        def _():
            combine(choose(table_step, j - 2))

        return 0

    lax.fori_loop(0, 2 * n_z, compute, 0)
    send_keys(0)
    combine(table_step[-2])
    combine(table_step[-1])

    pltpu.make_async_copy(dq_in.at[pl.ds(1, n_z - 1)], dq_in.at[pl.ds(1, n_z - 1)], dq_recv).wait()
    total = own_half[0]
    for i in range(1, n_z):
        total = total + dq_in[i].astype(F32)
    oq_ref[...] = total.astype(BF16)

    def settle(buf, n, sem):
        pltpu.make_async_copy(buf.at[pl.ds(0, n)], buf.at[pl.ds(0, n)], sem).wait()

    @pl.when(to_self)
    def _():
        settle(p_in, n_h - 1, p_recv)

    @pl.when(jnp.logical_not(to_self))
    def _():
        settle(p_in, n_h, p_recv)

    op_ref[...] = p_in[...]

    for way in (0, 1):
        near(way).wait_send()
        fourth(way).wait_send()
        for half in (0, 1):
            far(way, half).wait_send()
            third(way, half).wait_send()
    for i in range(n_z):
        pair(i).wait_send()
        swap_half(i).wait_send()
    settle(dq_out, n_z - 1, dq_send)

    @pl.when(to_self)
    def _():
        settle(p_out, slots * n_z - 1, p_send)
        settle(kvs, runs - 1, kv_send)

    @pl.when(jnp.logical_not(to_self))
    def _():
        settle(p_out, slots * n_z, p_send)

    @pl.when(is_source & jnp.logical_not(to_self))
    def _():
        settle(kvs, runs, kv_send)


def last_kernel(q_ref, p_ref, oq_ref, ok_ref, ov_ref, wide):
    n_h, both, _ = p_ref.shape
    dr = both // 2
    oq_ref[...] = q_ref[...]
    wide[...] = p_ref[...].astype(F32).reshape(n_h * both, LANES)
    for which, ref in enumerate((ok_ref, ov_ref)):
        picked = [wide[pl.ds(which * dr + d, n_h, stride=both), :] for d in range(dr)]
        ref[...] = jnp.concatenate(picked, 0).T.astype(BF16)


def on_device(kv_states, queries_t, grad_out_t, log_norm, delta, lengths):
    n_z, n_s = lax.axis_size("grp"), lax.axis_size("seq")
    n_h = n_s // 2
    rows, cols = kv_states.shape
    tokens = queries_t.shape[1]
    slots = n_h // n_z
    keys = slots * rows
    dr = DH // n_z
    hbm = pl.BlockSpec(memory_space=pl.ANY)
    vmem = pl.BlockSpec(memory_space=pltpu.VMEM)
    dma = pltpu.SemaphoreType.DMA
    grad_query, tiles = pl.pallas_call(
        functools.partial(kernel, n_z, n_h, rows * n_s),
        out_shape=(
            jax.ShapeDtypeStruct((HALF, tokens), BF16),
            jax.ShapeDtypeStruct((n_h, 2 * dr, LANES), BF16),
        ),
        in_specs=[hbm] * 5 + [pl.BlockSpec(memory_space=pltpu.SMEM)],
        out_specs=(vmem,) * 2,
        scratch_shapes=[
            pltpu.VMEM((rows, cols), BF16),
            pltpu.VMEM((n_h, tokens), F32),
            pltpu.VMEM((n_h, tokens), F32),
            pltpu.VMEM((n_h, rows, LANES), BF16),
            pltpu.VMEM((slots, rows, LANES), BF16),
            pltpu.VMEM((n_z, 2, PART, tokens), BF16),
            pltpu.VMEM((2, keys, 2 * PART), BF16),
            pltpu.VMEM((2, DH, keys // 2), BF16),
            pltpu.VMEM((keys, 2 * DH), F32),
            pltpu.VMEM((n_z, DH, tokens), F32),
            pltpu.VMEM((n_z, HALF, tokens), F32),
            pltpu.VMEM((n_z, HALF, tokens), F32),
            pltpu.VMEM((n_z, HALF, tokens), F32),
            pltpu.VMEM((n_z, HALF, tokens), BF16),
            pltpu.VMEM((n_z, HALF, tokens), BF16),
            pltpu.VMEM((slots * n_z, 2 * dr, LANES), BF16),
            pltpu.VMEM((n_h, 2 * dr, LANES), BF16),
            dma((5,)),
            dma, dma((slots,)),
            dma((2,)), dma((2,)),
            dma((2, 2)), dma((2, 2)),
            dma((2, 2)), dma((2, 2)),
            dma((2,)), dma((2,)),
            dma((n_z,)), dma((n_z,)),
            dma((n_z,)), dma((n_z,)),
            dma, dma, dma, dma,
        ],
        compiler_params=pltpu.CompilerParams(
            collective_id=0, has_side_effects=True, vmem_limit_bytes=63 * 1024 * 1024
        ),
        cost_estimate=pl.CostEstimate(
            flops=10 * DH * keys * tokens * n_z,
            bytes_accessed=4 * 1024 * 1024,
            transcendentals=keys * tokens * n_z,
        ),
    )(kv_states, queries_t, grad_out_t, log_norm, delta, lengths)
    return pl.pallas_call(
        last_kernel,
        out_shape=(
            jax.ShapeDtypeStruct((HALF, tokens), BF16),
            jax.ShapeDtypeStruct((rows, dr * n_h), BF16),
            jax.ShapeDtypeStruct((rows, dr * n_h), BF16),
        ),
        in_specs=[vmem] * 2,
        out_specs=(vmem,) * 3,
        scratch_shapes=[pltpu.VMEM((n_h * 2 * dr, LANES), F32)],
    )(grad_query, tiles)


def solution(mesh):
    placed = (
        P("seq", None),
        P("seq", "grp"),
        P("seq", "grp"),
        P(None, "grp"),
        P(None, "grp"),
        P("grp"),
    )
    return jax.shard_map(
        on_device,
        mesh=mesh,
        in_specs=placed,
        out_specs=(P("seq", "grp"), P("seq", "grp"), P("seq", "grp")),
        check_vma=False,
    )
```

```python
import functools
import math

import jax
import jax.numpy as jnp
from jax import lax
from jax.experimental import pallas as pl
from jax.experimental.pallas import tpu as pltpu
from jax.sharding import PartitionSpec as P

DH = 64
LEN = 256
HALF = DH // 2
STATS = 16
PART = 2 * HALF
DEPTH = 2 * PART + STATS
LANES = 128
MESH = pl.DeviceIdType.MESH
F32 = jnp.float32
BF16 = jnp.bfloat16

AWAY = (
    ((4, 3), (3, 2), (5, 2), (4, 2)),
    ((3, 3), (5, 1), (6, 2), (4, 1)),
    ((3, 1), (5, 3), (2, 2), (4, 0)),
    ((2, 3), (6, 1), (7, 2), (5, 0)),
    ((2, 1), (6, 3), (1, 2), (3, 0)),
    ((1, 1), (1, 3), (7, 1), (7, 3)),
    ((7, 0), (0, 2), (2, 0), (6, 0)),
    ((0, 0), (0, 1), (0, 3), (1, 0)),
)

NT = (((1,), (1,)), ((), ()))
NN = (((1,), (0,)), ((), ()))


def dot(a, b, dims=NN):
    return lax.dot_general(a, b, dims, preferred_element_type=F32)


def exchange_lanes(tiles, unit):
    count = len(tiles)
    lane = lax.broadcasted_iota(jnp.int32, tiles[0].shape, 1)
    step = 1
    while step < count:
        shift = step * unit
        low = (lane & shift) == 0
        made = list(tiles)
        for a in range(count):
            if a & step == 0:
                x, y = tiles[a], tiles[a | step]
                made[a] = jnp.where(low, x, pltpu.roll(y, shift, 1))
                made[a | step] = jnp.where(low, pltpu.roll(x, LANES - shift, 1), y)
        tiles = made
        step *= 2
    return tiles


def kernel(
    n_z, n_h, keys_all,
    kv_hbm, q_hbm, g_hbm, ln_hbm, dl_hbm, len_hbm,
    oq_ref, op_ref,
    kvx, lnv, dlv, len_ref, stored, stats, kvs, kvb, blocks, lhs, keys_t, acc,
    dq_sum, own_half, sent_half, got_half, dq_out, dq_in, p_out, dq_done,
    in_sem, out_sem, stat_send, stat_recv, kv_send, kv_recv, near_send, near_recv, far_send, far_recv,
    third_send, third_recv, fourth_send, fourth_recv, pair_send, pair_recv,
    half_send, half_recv, dq_send, dq_recv, p_send, p_recv,
):
    z = lax.axis_index("grp")
    s = lax.axis_index("seq")
    h = s // 2
    c = s - 2 * h
    partner = 2 * h + 1 - c
    rows = kvx.shape[0]
    tokens = blocks.shape[3]
    span = tokens // 2
    slots = kvb.shape[0]
    chunk = slots * rows // 2
    dr = DH // n_z

    width = n_z // 2
    runs = n_h // width
    run = h // width
    along_run = h - run * width
    to_self = z == n_z - 1

    def choose(table, i):
        out = jnp.int32(table[-1])
        for k in range(len(table) - 1):
            out = jnp.where(i == k, table[k], out)
        return out

    sources, served = [], []
    for place in range(slots):
        down = choose([AWAY[k][place][0] for k in range(n_z)], z)
        right = choose([AWAY[k][place][1] for k in range(n_z)], z)
        sources.append(lax.rem(run + down, runs) * width + lax.rem(along_run + right, width))
        served.append(
            lax.rem(run + runs - down, runs) * width + lax.rem(along_run + width - right, width)
        )

    def unless_self(place, go):
        if place == 0:
            pl.when(jnp.logical_not(to_self))(go)
        else:
            go()

    barrier = pltpu.get_barrier_semaphore()

    def greet(device):
        pl.semaphore_signal(barrier, inc=1, device_id=device, device_id_type=MESH)

    def greet_line(i, _):
        greet((lax.rem(z + i, n_z), s))
        return 0

    for place in range(slots):
        unless_self(place, functools.partial(greet, (z, 2 * sources[place] + c)))
    lax.fori_loop(1, n_z, greet_line, 0)
    greet((z, partner))

    loads = [
        pltpu.make_async_copy(ln_hbm, lnv, in_sem.at[0]),
        pltpu.make_async_copy(dl_hbm, dlv, in_sem.at[1]),
        pltpu.make_async_copy(q_hbm, blocks.at[z, c, pl.ds(0, HALF)], in_sem.at[2]),
        pltpu.make_async_copy(g_hbm, blocks.at[z, c, pl.ds(HALF, HALF)], in_sem.at[3]),
    ]
    for load in loads:
        load.start()
    load_lengths = pltpu.make_async_copy(len_hbm, len_ref, in_sem.at[5])
    load_lengths.start()
    load_kv = pltpu.make_async_copy(kv_hbm, kvx, in_sem.at[4])

    load_kv.start()

    loads[0].wait()
    loads[1].wait()
    load_lengths.wait()
    place = lax.broadcasted_iota(jnp.int32, (1, tokens), 1)
    limit = jnp.zeros((1, tokens), jnp.int32)
    for a in range(tokens // LEN):
        limit = jnp.where(place // LEN == a, len_ref[a], limit)
    norm = -(lnv[pl.ds(h, 1), :] + math.log(keys_all))
    norm = jnp.where(lax.rem(place, LEN) < limit, norm, -1e30)
    less = -dlv[pl.ds(h, 1), :]
    for k in range(tokens // LANES):
        columns = slice(k * LANES, (k + 1) * LANES)
        stored[z, k : k + 1] = norm[:, columns]
        stored[z, tokens // LANES + k : tokens // LANES + k + 1] = less[:, columns]
    loads[2].wait()
    loads[3].wait()

    load_kv.wait()

    group = LANES // slots
    at = lax.broadcasted_iota(jnp.int32, (2 * LANES, LANES), 0)
    to = lax.broadcasted_iota(jnp.int32, (2 * LANES, LANES), 1)
    wanted = jnp.zeros_like(to)
    for place in range(slots):
        wanted = jnp.where(to // group == place, served[place], wanted)
    by_head = lax.rem(at, n_h) == wanted
    per = 2 * LANES // n_h
    picked = jnp.zeros((slots * rows, LANES), F32)
    for step in range(group // per):
        one_hot = by_head & (lax.rem(to, group) == step * per + at // n_h)
        taken = [
            kvx[:, (m * group // per + step) * 2 * LANES : (m * group // per + step + 1) * 2 * LANES]
            for m in range(slots)
        ]
        picked += dot(jnp.concatenate(taken, 0), jnp.where(one_hot, 1.0, 0.0).astype(BF16))
    tiles = exchange_lanes([picked[m * rows : (m + 1) * rows] for m in range(slots)], group)
    for place in range(slots):
        kvs[place] = tiles[place].astype(BF16)

    @pl.when(to_self)
    def _():
        kvb[0] = kvs[0]

    pl.semaphore_wait(barrier, n_z + slots - jnp.where(to_self, 1, 0))

    every = pl.ds(0, tokens)

    def columns_of(half):
        return pl.ds(pl.multiple_of(half * span, span), span)


    def order(i):
        t = (i + 1) // 2
        return lax.rem(jnp.where(lax.rem(i, 2) == 1, z - t, z + t) + n_z, n_z)

    def along(way, hops, block, columns, send, recv):
        to = lax.rem(z + jnp.where(way == 0, hops, n_z - hops), n_z)
        ref = blocks.at[block, c, :, columns]
        return pltpu.make_async_remote_copy(
            src_ref=ref, dst_ref=ref, send_sem=send, recv_sem=recv,
            device_id=(to, s), device_id_type=MESH,
        )

    def near(way):
        return along(way, 1, z, every, near_send.at[way], near_recv.at[way])

    def far(way, half):
        return along(way, 2, z, columns_of(half), far_send.at[way, half], far_recv.at[way, half])

    def third(way, half):
        block = order(3 + way)
        return along(way, 1, block, columns_of(half), third_send.at[way, half], third_recv.at[way, half])

    def fourth(way):
        return along(way, 2, order(3 + way), columns_of(way), fourth_send.at[way], fourth_recv.at[way])

    def pair(i):
        ref = blocks.at[order(i), c]
        return pltpu.make_async_remote_copy(
            src_ref=ref, dst_ref=ref,
            send_sem=pair_send.at[i], recv_sem=pair_recv.at[i],
            device_id=(z, partner), device_id_type=MESH,
        )

    for half in (0, 1):
        for way in (0, 1):
            far(way, half).start()

    def send_stored(i, _):
        pltpu.make_async_remote_copy(
            src_ref=stored.at[z], dst_ref=stored.at[z], send_sem=stat_send, recv_sem=stat_recv,
            device_id=(lax.rem(z + i, n_z), s), device_id_type=MESH,
        ).start()
        return 0

    for way in (0, 1):
        near(way).start()
    lax.fori_loop(1, n_z, send_stored, 0)
    pair(0).start()

    for place in reversed(range(slots)):
        copy = pltpu.make_async_remote_copy(
            src_ref=kvs.at[place], dst_ref=kvb.at[place],
            send_sem=kv_send.at[place], recv_sem=kv_recv.at[place],
            device_id=(z, 2 * served[place] + c), device_id_type=MESH,
        )
        unless_self(place, copy.start)

    lane = lax.broadcasted_iota(jnp.int32, (LANES, DEPTH), 0)
    col = lax.broadcasted_iota(jnp.int32, (LANES, DEPTH), 1)
    side = col // PART
    within = col - side * PART
    is_key = (side < 2) & (within < HALF)
    is_value = (side < 2) & (within >= HALF)
    for_scores = jnp.where(is_key & (lane == side * HALF + within), 1.0, 0.0).astype(BF16)
    for_dprobs = jnp.where(
        is_value & (lane == DH + side * HALF + within - HALF), 1.0, 0.0
    ).astype(BF16)
    one = lax.broadcasted_iota(jnp.int32, (1, DEPTH), 1) - 2 * PART
    ones_s = jnp.where((one >= 0) & (one < 3), 1.0, 0.0)
    ones_p = jnp.where((one >= 3) & (one < 6), 1.0, 0.0)
    lane_t = lax.broadcasted_iota(jnp.int32, (DH, LANES), 1)
    row_t = lax.broadcasted_iota(jnp.int32, (DH, LANES), 0)
    for_keys = jnp.where(lane_t == row_t, 1.0, 0.0).astype(BF16)
    acc[...] = jnp.zeros_like(acc)

    first_way = jnp.where((z >= n_z // 4) & (z < 3 * n_z // 4), 0, 1)
    for half in (0, 1):
        for way in (first_way, 1 - first_way):
            far(way, half).wait_recv()
            third(way, half).start()

            @pl.when(way == half)
            def _():
                fourth(way).start()

    for way in (0, 1):
        pair(3 + way).start()
    for way in (0, 1):
        near(way).wait_recv()
        pair(1 + way).start()

    pltpu.make_async_copy(stored.at[pl.ds(1, n_z - 1)], stored.at[pl.ds(1, n_z - 1)], stat_recv).wait()
    at = lax.broadcasted_iota(jnp.int32, (STATS, tokens), 0)

    def split(b, _):
        rows_of = tokens // LANES
        norm = jnp.concatenate([stored[b, k : k + 1] for k in range(rows_of)], 1)
        less = jnp.concatenate([stored[b, rows_of + k : rows_of + k + 1] for k in range(rows_of)], 1)
        both = jnp.where(at < 3, norm, less)
        high = both.astype(BF16).astype(F32)
        middle = (both - high).astype(BF16).astype(F32)
        low = both - high - middle
        which = lax.rem(at, 3)
        out = jnp.where(which == 0, high, jnp.where(which == 1, middle, low))
        stats[b] = jnp.where(at < 6, out, 0.0).astype(BF16)
        return 0

    lax.fori_loop(0, n_z, split, 0)

    def keys_in(part):
        for place in (part * slots // 2, part * slots // 2 + 1):

            arrived = pltpu.make_async_copy(kvb.at[place], kvb.at[place], kv_recv.at[place])
            unless_self(place, arrived.wait)

        at = pl.ds(part * chunk, chunk)
        mixed = kvb[pl.ds(part * slots // 2, slots // 2)].reshape(chunk, LANES)
        lhs[0, at] = (dot(mixed, for_scores) + ones_s).astype(BF16)
        lhs[1, at] = (dot(mixed, for_dprobs) + ones_p).astype(BF16)
        keys_t[part] = dot(for_keys, mixed, NT).astype(BF16)

    keys_in(0)

    def swap_half(i):
        return pltpu.make_async_remote_copy(
            src_ref=sent_half.at[i], dst_ref=got_half.at[i],
            send_sem=half_send.at[i], recv_sem=half_recv.at[i],
            device_id=(z, partner), device_id_type=MESH,
        )

    def dq_copy(i):
        return pltpu.make_async_remote_copy(
            src_ref=dq_out.at[i], dst_ref=dq_in.at[i], send_sem=dq_send, recv_sem=dq_recv,
            device_id=(order(i), s), device_id_type=MESH,
        )

    def combine(i):
        swap_half(i).wait_recv()
        total = own_half[i] + got_half[i]
        own_half[i] = total
        dq_out[i] = total.astype(BF16)

        @pl.when(i > 0)
        def _():
            dq_copy(i).start()

    own_tile = pltpu.make_async_copy(p_out.at[z], op_ref.at[h], out_sem.at[0])
    out_query = pltpu.make_async_copy(dq_done, oq_ref, out_sem.at[1])

    def send_keys(part):
        turned = acc[part * chunk : (part + 1) * chunk].T.reshape(2, n_z, dr, chunk)
        first = part * slots // 2
        for place in range(slots // 2):
            columns = slice(place * rows, (place + 1) * rows)
            for g in range(n_z):
                tile = jnp.concatenate([turned[0, g, :, columns], turned[1, g, :, columns]], 0)
                p_out[(first + place) * n_z + g] = tile.astype(BF16)
        if part == 0:
            pl.when(to_self)(own_tile.start)

        for place in reversed(range(first, first + slots // 2)):

            def send(g, _):
                def go():
                    pltpu.make_async_remote_copy(
                        src_ref=p_out.at[place * n_z + g], dst_ref=op_ref.at[h],
                        send_sem=p_send, recv_sem=p_recv,
                        device_id=(g, 2 * sources[place] + c), device_id_type=MESH,
                    ).start()

                if place == 0:
                    pl.when(jnp.logical_not(to_self & (g == z)))(go)
                else:
                    go()
                return 0

            lax.fori_loop(0, n_z, send, 0)

    table_part = (0,) * 5 + (1,) * 8 + (0,) * 3
    table_step = (0, 1, 2, 3, 4, 0, 1, 2, 3, 4, 5, 6, 7, 5, 6, 7)
    table_ends = (0,) * 5 + (1,) * 5 + (0,) * 3 + (1,) * 3
    keys_at, third_at, fourth_at, far_done = 0, 5, 7, 13

    def compute(j, _):
        part = choose(table_part, j)
        i = choose(table_step, j)
        opens = choose(table_ends, j) == 0

        @pl.when(j == keys_at)
        def _():
            keys_in(1)

        @pl.when(j == third_at)
        def _():
            for way in (0, 1):
                for half in (0, 1):
                    third(way, half).wait_recv()
                pair(5 + way).start()

        @pl.when(j == fourth_at)
        def _():
            for way in (0, 1):
                fourth(way).wait_recv()
            pair(7).start()

        @pl.when(j == far_done)
        def _():
            send_keys(1)

        block = order(i)

        @pl.when(opens)
        def _():
            pltpu.make_async_copy(
                blocks.at[block, 1 - c], blocks.at[block, 1 - c], pair_recv.at[i]
            ).wait()

        rhs = jnp.concatenate([blocks[block].reshape(2 * PART, tokens), stats[block]], 0)
        blank = jnp.zeros((DH, tokens), BF16)
        q_rows = jnp.concatenate([rhs[:HALF], rhs[PART : PART + HALF], blank], 0)
        g_rows = jnp.concatenate([blank, rhs[HALF:PART], rhs[PART + HALF : 2 * PART]], 0)
        at = pl.ds(pl.multiple_of(part * chunk, chunk), chunk)
        probs = jnp.exp(dot(lhs[0, at], rhs))
        dscores = probs * dot(lhs[1, at], rhs)
        probs = probs.astype(BF16)
        dscores = dscores.astype(BF16)
        acc[at] += dot(dscores, q_rows, NT) + dot(probs, g_rows, NT)
        dq = dot(keys_t[part], dscores)

        @pl.when(opens)
        def _():
            dq_sum[i] = dq

        @pl.when(jnp.logical_not(opens))
        def _():
            total = dq_sum[i] + dq
            top, bottom = total[:HALF], total[HALF:]
            own_half[i] = jnp.where(c == 0, top, bottom)
            sent_half[i] = jnp.where(c == 0, bottom, top)
            swap_half(i).start()

        @pl.when((j >= 2) & (choose(table_ends, j - 2) == 1))
        def _():
            combine(choose(table_step, j - 2))

        return 0

    lax.fori_loop(0, 2 * n_z, compute, 0)
    send_keys(0)
    combine(table_step[-2])
    combine(table_step[-1])

    pltpu.make_async_copy(dq_in.at[pl.ds(1, n_z - 1)], dq_in.at[pl.ds(1, n_z - 1)], dq_recv).wait()
    total = own_half[0]
    for i in range(1, n_z):
        total = total + dq_in[i].astype(F32)
    dq_done[...] = total.astype(BF16)
    out_query.start()

    def settle(buf, n, sem):
        pltpu.make_async_copy(buf.at[pl.ds(0, n)], buf.at[pl.ds(0, n)], sem).wait()

    @pl.when(to_self)
    def _():
        settle(op_ref, n_h - 1, p_recv)
        own_tile.wait()

    @pl.when(jnp.logical_not(to_self))
    def _():
        settle(op_ref, n_h, p_recv)

    out_query.wait()

    for way in (0, 1):
        near(way).wait_send()
        fourth(way).wait_send()
        for half in (0, 1):
            far(way, half).wait_send()
            third(way, half).wait_send()
    for i in range(n_z):
        pair(i).wait_send()
        swap_half(i).wait_send()
    settle(dq_out, n_z - 1, dq_send)
    settle(stored, n_z - 1, stat_send)

    @pl.when(to_self)
    def _():
        settle(p_out, slots * n_z - 1, p_send)

    @pl.when(jnp.logical_not(to_self))
    def _():
        settle(p_out, slots * n_z, p_send)

    for place in range(slots):
        left = pltpu.make_async_copy(kvb.at[place], kvb.at[place], kv_send.at[place])
        unless_self(place, left.wait)


def last_kernel(q_ref, p_ref, oq_ref, ok_ref, ov_ref, wide):
    n_h, both, _ = p_ref.shape
    dr = both // 2
    oq_ref[...] = q_ref[...]
    wide[...] = p_ref[...].astype(F32).reshape(n_h * both, LANES)
    for which, ref in enumerate((ok_ref, ov_ref)):
        picked = [wide[pl.ds(which * dr + d, n_h, stride=both), :] for d in range(dr)]
        ref[...] = jnp.concatenate(picked, 0).T.astype(BF16)


def on_device(kv_states, queries_t, grad_out_t, log_norm, delta, lengths):
    n_z, n_s = lax.axis_size("grp"), lax.axis_size("seq")
    n_h = n_s // 2
    rows, cols = kv_states.shape
    tokens = queries_t.shape[1]
    slots = n_h // n_z
    keys = slots * rows
    dr = DH // n_z
    given = (kv_states, queries_t, grad_out_t, log_norm, delta, lengths)
    hbm = pl.BlockSpec(memory_space=pl.ANY)
    vmem = pl.BlockSpec(memory_space=pltpu.VMEM)
    dma = pltpu.SemaphoreType.DMA
    grad_query, tiles = pl.pallas_call(
        functools.partial(kernel, n_z, n_h, rows * n_s),
        out_shape=(
            jax.ShapeDtypeStruct((HALF, tokens), BF16),
            jax.ShapeDtypeStruct((n_h, 2 * dr, LANES), BF16),
        ),
        in_specs=[hbm] * 6,
        out_specs=(hbm,) * 2,
        scratch_shapes=[
            pltpu.VMEM((rows, cols), BF16),
            pltpu.VMEM((n_h, tokens), F32),
            pltpu.VMEM((n_h, tokens), F32),
            pltpu.SMEM(lengths.shape, jnp.int32),
            pltpu.VMEM((n_z, 2 * tokens // LANES, LANES), F32),
            pltpu.VMEM((n_z, STATS, tokens), BF16),
            pltpu.VMEM((slots, rows, LANES), BF16),
            pltpu.VMEM((slots, rows, LANES), BF16),
            pltpu.VMEM((n_z, 2, PART, tokens), BF16),
            pltpu.VMEM((2, keys, DEPTH), BF16),
            pltpu.VMEM((2, DH, keys // 2), BF16),
            pltpu.VMEM((keys, 2 * DH), F32),
            pltpu.VMEM((n_z, DH, tokens), F32),
            pltpu.VMEM((n_z, HALF, tokens), F32),
            pltpu.VMEM((n_z, HALF, tokens), F32),
            pltpu.VMEM((n_z, HALF, tokens), F32),
            pltpu.VMEM((n_z, HALF, tokens), BF16),
            pltpu.VMEM((n_z, HALF, tokens), BF16),
            pltpu.VMEM((slots * n_z, 2 * dr, LANES), BF16),
            pltpu.VMEM((HALF, tokens), BF16),
            dma((6,)), dma((2,)),
            dma, dma,
            dma((slots,)), dma((slots,)),
            dma((2,)), dma((2,)),
            dma((2, 2)), dma((2, 2)),
            dma((2, 2)), dma((2, 2)),
            dma((2,)), dma((2,)),
            dma((n_z,)), dma((n_z,)),
            dma((n_z,)), dma((n_z,)),
            dma, dma, dma, dma,
        ],
        compiler_params=pltpu.CompilerParams(
            collective_id=0, has_side_effects=True, vmem_limit_bytes=63 * 1024 * 1024
        ),
        cost_estimate=pl.CostEstimate(
            flops=10 * DH * keys * tokens * n_z,
            bytes_accessed=4 * 1024 * 1024,
            transcendentals=keys * tokens * n_z,
        ),
    )(*given)
    return pl.pallas_call(
        last_kernel,
        out_shape=(
            jax.ShapeDtypeStruct((HALF, tokens), BF16),
            jax.ShapeDtypeStruct((rows, dr * n_h), BF16),
            jax.ShapeDtypeStruct((rows, dr * n_h), BF16),
        ),
        in_specs=[vmem] * 2,
        out_specs=(vmem,) * 3,
        scratch_shapes=[pltpu.VMEM((n_h * 2 * dr, LANES), F32)],
    )(grad_query, tiles)


def solution(mesh):
    placed = (
        P("seq", None),
        P("seq", "grp"),
        P("seq", "grp"),
        P(None, "grp"),
        P(None, "grp"),
        P("grp"),
    )
    return jax.shard_map(
        on_device,
        mesh=mesh,
        in_specs=placed,
        out_specs=(P("seq", "grp"), P("seq", "grp"), P("seq", "grp")),
        check_vma=False,
    )
```

```python
import functools
import math

import jax
import jax.numpy as jnp
from jax import lax
from jax.experimental import pallas as pl
from jax.experimental.pallas import tpu as pltpu
from jax.sharding import PartitionSpec as P

DH = 64
LEN = 256
HALF = DH // 2
STATS = 16
PART = 2 * HALF
DEPTH = 2 * PART + STATS
LANES = 128
MESH = pl.DeviceIdType.MESH
F32 = jnp.float32
BF16 = jnp.bfloat16

AWAY = (
    ((4, 3), (3, 2), (5, 2), (4, 2)),
    ((3, 3), (5, 1), (6, 2), (4, 1)),
    ((3, 1), (5, 3), (2, 2), (4, 0)),
    ((2, 3), (6, 1), (7, 2), (5, 0)),
    ((2, 1), (6, 3), (1, 2), (3, 0)),
    ((1, 1), (1, 3), (7, 1), (7, 3)),
    ((7, 0), (0, 2), (2, 0), (6, 0)),
    ((0, 0), (0, 1), (0, 3), (1, 0)),
)

NT = (((1,), (1,)), ((), ()))
NN = (((1,), (0,)), ((), ()))


def dot(a, b, dims=NN):
    return lax.dot_general(a, b, dims, preferred_element_type=F32)


def exchange_lanes(tiles, unit):
    count = len(tiles)
    lane = lax.broadcasted_iota(jnp.int32, tiles[0].shape, 1)
    step = 1
    while step < count:
        shift = step * unit
        low = (lane & shift) == 0
        made = list(tiles)
        for a in range(count):
            if a & step == 0:
                x, y = tiles[a], tiles[a | step]
                made[a] = jnp.where(low, x, pltpu.roll(y, shift, 1))
                made[a | step] = jnp.where(low, pltpu.roll(x, LANES - shift, 1), y)
        tiles = made
        step *= 2
    return tiles


def kernel(
    n_z, n_h, keys_all,
    kv_hbm, q_hbm, g_hbm, ln_hbm, dl_hbm, len_hbm,
    oq_ref, op_ref,
    kvx, lnv, dlv, len_ref, stored, stats, kvs, kvb, blocks, lhs, keys_t, acc,
    dq_sum, own_half, sent_half, got_half, dq_out, dq_in, p_out, dq_done,
    in_sem, out_sem, stat_send, stat_recv, kv_send, kv_recv, near_send, near_recv, far_send, far_recv,
    third_send, third_recv, fourth_send, fourth_recv, pair_send, pair_recv,
    half_send, half_recv, dq_send, dq_recv, p_send, p_recv,
):
    z = lax.axis_index("grp")
    s = lax.axis_index("seq")
    h = s // 2
    c = s - 2 * h
    partner = 2 * h + 1 - c
    rows = kvx.shape[0]
    tokens = blocks.shape[3]
    span = tokens // 2
    slots = kvb.shape[0]
    chunk = slots * rows // 2
    dr = DH // n_z

    width = n_z // 2
    runs = n_h // width
    run = h // width
    along_run = h - run * width
    to_self = z == n_z - 1

    def choose(table, i):
        out = jnp.int32(table[-1])
        for k in range(len(table) - 1):
            out = jnp.where(i == k, table[k], out)
        return out

    sources, served = [], []
    for place in range(slots):
        down = choose([AWAY[k][place][0] for k in range(n_z)], z)
        right = choose([AWAY[k][place][1] for k in range(n_z)], z)
        sources.append(lax.rem(run + down, runs) * width + lax.rem(along_run + right, width))
        served.append(
            lax.rem(run + runs - down, runs) * width + lax.rem(along_run + width - right, width)
        )

    def unless_self(place, go):
        if place == 0:
            pl.when(jnp.logical_not(to_self))(go)
        else:
            go()

    barrier = pltpu.get_barrier_semaphore()

    def greet(device):
        pl.semaphore_signal(barrier, inc=1, device_id=device, device_id_type=MESH)

    def greet_line(i, _):
        greet((lax.rem(z + i, n_z), s))
        return 0

    for place in range(slots):
        unless_self(place, functools.partial(greet, (z, 2 * sources[place] + c)))
    lax.fori_loop(1, n_z, greet_line, 0)
    greet((z, partner))

    loads = [
        pltpu.make_async_copy(ln_hbm, lnv, in_sem.at[0]),
        pltpu.make_async_copy(dl_hbm, dlv, in_sem.at[1]),
        pltpu.make_async_copy(q_hbm, blocks.at[z, c, pl.ds(0, HALF)], in_sem.at[2]),
        pltpu.make_async_copy(g_hbm, blocks.at[z, c, pl.ds(HALF, HALF)], in_sem.at[3]),
    ]
    for load in loads:
        load.start()
    load_lengths = pltpu.make_async_copy(len_hbm, len_ref, in_sem.at[5])
    load_lengths.start()
    load_kv = pltpu.make_async_copy(kv_hbm, kvx, in_sem.at[4])

    load_kv.start()

    loads[0].wait()
    loads[1].wait()
    load_lengths.wait()
    place = lax.broadcasted_iota(jnp.int32, (1, tokens), 1)
    limit = jnp.zeros((1, tokens), jnp.int32)
    for a in range(tokens // LEN):
        limit = jnp.where(place // LEN == a, len_ref[a], limit)
    norm = -(lnv[pl.ds(h, 1), :] + math.log(keys_all))
    norm = jnp.where(lax.rem(place, LEN) < limit, norm, -1e30)
    less = -dlv[pl.ds(h, 1), :]
    for k in range(tokens // LANES):
        columns = slice(k * LANES, (k + 1) * LANES)
        stored[z, k : k + 1] = norm[:, columns]
        stored[z, tokens // LANES + k : tokens // LANES + k + 1] = less[:, columns]
    loads[2].wait()
    loads[3].wait()

    load_kv.wait()

    group = LANES // slots
    at = lax.broadcasted_iota(jnp.int32, (2 * LANES, LANES), 0)
    to = lax.broadcasted_iota(jnp.int32, (2 * LANES, LANES), 1)
    wanted = jnp.zeros_like(to)
    for place in range(slots):
        wanted = jnp.where(to // group == place, served[place], wanted)
    by_head = lax.rem(at, n_h) == wanted
    per = 2 * LANES // n_h
    picked = jnp.zeros((slots * rows, LANES), F32)
    for step in range(group // per):
        one_hot = by_head & (lax.rem(to, group) == step * per + at // n_h)
        taken = [
            kvx[:, (m * group // per + step) * 2 * LANES : (m * group // per + step + 1) * 2 * LANES]
            for m in range(slots)
        ]
        picked += dot(jnp.concatenate(taken, 0), jnp.where(one_hot, 1.0, 0.0).astype(BF16))
    tiles = exchange_lanes([picked[m * rows : (m + 1) * rows] for m in range(slots)], group)
    for place in range(slots):
        kvs[place] = tiles[place].astype(BF16)

    @pl.when(to_self)
    def _():
        kvb[0] = kvs[0]

    pl.semaphore_wait(barrier, n_z + slots - jnp.where(to_self, 1, 0))

    every = pl.ds(0, tokens)

    def columns_of(half):
        return pl.ds(pl.multiple_of(half * span, span), span)


    def order(i):
        t = (i + 1) // 2
        return lax.rem(jnp.where(lax.rem(i, 2) == 1, z - t, z + t) + n_z, n_z)

    def along(way, hops, block, columns, send, recv):
        to = lax.rem(z + jnp.where(way == 0, hops, n_z - hops), n_z)
        ref = blocks.at[block, c, :, columns]
        return pltpu.make_async_remote_copy(
            src_ref=ref, dst_ref=ref, send_sem=send, recv_sem=recv,
            device_id=(to, s), device_id_type=MESH,
        )

    def near(way):
        return along(way, 1, z, every, near_send.at[way], near_recv.at[way])

    def far(way, half):
        return along(way, 2, z, columns_of(half), far_send.at[way, half], far_recv.at[way, half])

    def third(way, half):
        block = order(3 + way)
        return along(way, 1, block, columns_of(half), third_send.at[way, half], third_recv.at[way, half])

    def fourth(way):
        return along(way, 2, order(3 + way), columns_of(way), fourth_send.at[way], fourth_recv.at[way])

    def pair(i):
        ref = blocks.at[order(i), c]
        return pltpu.make_async_remote_copy(
            src_ref=ref, dst_ref=ref,
            send_sem=pair_send.at[i], recv_sem=pair_recv.at[i],
            device_id=(z, partner), device_id_type=MESH,
        )

    for half in (0, 1):
        for way in (0, 1):
            far(way, half).start()

    def send_stored(i, _):
        pltpu.make_async_remote_copy(
            src_ref=stored.at[z], dst_ref=stored.at[z], send_sem=stat_send, recv_sem=stat_recv,
            device_id=(lax.rem(z + i, n_z), s), device_id_type=MESH,
        ).start()
        return 0

    for way in (0, 1):
        near(way).start()
    lax.fori_loop(1, n_z, send_stored, 0)
    pair(0).start()

    for place in reversed(range(slots)):
        copy = pltpu.make_async_remote_copy(
            src_ref=kvs.at[place], dst_ref=kvb.at[place],
            send_sem=kv_send.at[place], recv_sem=kv_recv.at[place],
            device_id=(z, 2 * served[place] + c), device_id_type=MESH,
        )
        unless_self(place, copy.start)

    lane = lax.broadcasted_iota(jnp.int32, (LANES, DEPTH), 0)
    col = lax.broadcasted_iota(jnp.int32, (LANES, DEPTH), 1)
    side = col // PART
    within = col - side * PART
    is_key = (side < 2) & (within < HALF)
    is_value = (side < 2) & (within >= HALF)
    for_scores = jnp.where(is_key & (lane == side * HALF + within), 1.0, 0.0).astype(BF16)
    for_dprobs = jnp.where(
        is_value & (lane == DH + side * HALF + within - HALF), 1.0, 0.0
    ).astype(BF16)
    one = lax.broadcasted_iota(jnp.int32, (1, DEPTH), 1) - 2 * PART
    ones_s = jnp.where((one >= 0) & (one < 3), 1.0, 0.0)
    ones_p = jnp.where((one >= 3) & (one < 6), 1.0, 0.0)
    lane_t = lax.broadcasted_iota(jnp.int32, (DH, LANES), 1)
    row_t = lax.broadcasted_iota(jnp.int32, (DH, LANES), 0)
    for_keys = jnp.where(lane_t == row_t, 1.0, 0.0).astype(BF16)
    acc[...] = jnp.zeros_like(acc)

    first_way = jnp.where((z >= n_z // 4) & (z < 3 * n_z // 4), 0, 1)
    for half in (0, 1):
        for way in (first_way, 1 - first_way):
            far(way, half).wait_recv()
            third(way, half).start()

            @pl.when(way == half)
            def _():
                fourth(way).start()

    for way in (0, 1):
        pair(3 + way).start()
    for way in (0, 1):
        near(way).wait_recv()
        pair(1 + way).start()

    pltpu.make_async_copy(stored.at[pl.ds(1, n_z - 1)], stored.at[pl.ds(1, n_z - 1)], stat_recv).wait()
    at = lax.broadcasted_iota(jnp.int32, (STATS, tokens), 0)

    def split(b, _):
        rows_of = tokens // LANES
        norm = jnp.concatenate([stored[b, k : k + 1] for k in range(rows_of)], 1)
        less = jnp.concatenate([stored[b, rows_of + k : rows_of + k + 1] for k in range(rows_of)], 1)
        both = jnp.where(at < 3, norm, less)
        high = both.astype(BF16).astype(F32)
        middle = (both - high).astype(BF16).astype(F32)
        low = both - high - middle
        which = lax.rem(at, 3)
        out = jnp.where(which == 0, high, jnp.where(which == 1, middle, low))
        stats[b] = jnp.where(at < 6, out, 0.0).astype(BF16)
        return 0

    lax.fori_loop(0, n_z, split, 0)

    def keys_in(part):
        for place in (part * slots // 2, part * slots // 2 + 1):

            arrived = pltpu.make_async_copy(kvb.at[place], kvb.at[place], kv_recv.at[place])
            unless_self(place, arrived.wait)

        at = pl.ds(part * chunk, chunk)
        mixed = kvb[pl.ds(part * slots // 2, slots // 2)].reshape(chunk, LANES)
        lhs[0, at] = (dot(mixed, for_scores) + ones_s).astype(BF16)
        lhs[1, at] = (dot(mixed, for_dprobs) + ones_p).astype(BF16)
        keys_t[part] = dot(for_keys, mixed, NT).astype(BF16)

    keys_in(0)

    def swap_half(i):
        return pltpu.make_async_remote_copy(
            src_ref=sent_half.at[i], dst_ref=got_half.at[i],
            send_sem=half_send.at[i], recv_sem=half_recv.at[i],
            device_id=(z, partner), device_id_type=MESH,
        )

    def dq_copy(i):
        return pltpu.make_async_remote_copy(
            src_ref=dq_out.at[i], dst_ref=dq_in.at[i], send_sem=dq_send, recv_sem=dq_recv,
            device_id=(order(i), s), device_id_type=MESH,
        )

    def combine(i):
        swap_half(i).wait_recv()
        total = own_half[i] + got_half[i]
        own_half[i] = total
        dq_out[i] = total.astype(BF16)

        @pl.when(i > 0)
        def _():
            dq_copy(i).start()

    own_tile = pltpu.make_async_copy(p_out.at[z], op_ref.at[h], out_sem.at[0])
    out_query = pltpu.make_async_copy(dq_done, oq_ref, out_sem.at[1])

    def send_keys(part):
        turned = acc[part * chunk : (part + 1) * chunk].T.reshape(2, n_z, dr, chunk)
        first = part * slots // 2
        for place in range(slots // 2):
            columns = slice(place * rows, (place + 1) * rows)
            for g in range(n_z):
                tile = jnp.concatenate([turned[0, g, :, columns], turned[1, g, :, columns]], 0)
                p_out[(first + place) * n_z + g] = tile.astype(BF16)
        if part == 0:
            pl.when(to_self)(own_tile.start)

        for place in reversed(range(first, first + slots // 2)):

            def send(g, _):
                def go():
                    pltpu.make_async_remote_copy(
                        src_ref=p_out.at[place * n_z + g], dst_ref=op_ref.at[h],
                        send_sem=p_send, recv_sem=p_recv,
                        device_id=(g, 2 * sources[place] + c), device_id_type=MESH,
                    ).start()

                if place == 0:
                    pl.when(jnp.logical_not(to_self & (g == z)))(go)
                else:
                    go()
                return 0

            lax.fori_loop(0, n_z, send, 0)

    early = 5

    def step_of(j):
        i = jnp.where(j < early, j, jnp.where(j < early + n_z, j - early, j - n_z))
        return i, ((j >= early) & (j < 2 * early)) | (j >= n_z + early)

    keys_at, third_at, fourth_at, far_done = 0, 5, 7, 13

    def compute(j, _):
        part = jnp.where((j >= early) & (j < early + n_z), 1, 0)
        i, ends = step_of(j)
        opens = jnp.logical_not(ends)
        before, ended = step_of(j - 2)

        @pl.when(j == keys_at)
        def _():
            keys_in(1)

        @pl.when(j == third_at)
        def _():
            for way in (0, 1):
                for half in (0, 1):
                    third(way, half).wait_recv()
                pair(5 + way).start()

        @pl.when(j == fourth_at)
        def _():
            for way in (0, 1):
                fourth(way).wait_recv()
            pair(7).start()

        @pl.when(j == far_done)
        def _():
            send_keys(1)

        block = order(i)

        @pl.when(opens)
        def _():
            pltpu.make_async_copy(
                blocks.at[block, 1 - c], blocks.at[block, 1 - c], pair_recv.at[i]
            ).wait()

        rhs = jnp.concatenate([blocks[block].reshape(2 * PART, tokens), stats[block]], 0)
        blank = jnp.zeros((DH, tokens), BF16)
        q_rows = jnp.concatenate([rhs[:HALF], rhs[PART : PART + HALF], blank], 0)
        g_rows = jnp.concatenate([blank, rhs[HALF:PART], rhs[PART + HALF : 2 * PART]], 0)
        at = pl.ds(pl.multiple_of(part * chunk, chunk), chunk)
        probs = jnp.exp(dot(lhs[0, at], rhs))
        dscores = probs * dot(lhs[1, at], rhs)
        probs = probs.astype(BF16)
        dscores = dscores.astype(BF16)
        acc[at] += dot(dscores, q_rows, NT) + dot(probs, g_rows, NT)
        dq = dot(keys_t[part], dscores)

        @pl.when(opens)
        def _():
            dq_sum[i] = dq

        @pl.when(jnp.logical_not(opens))
        def _():
            total = dq_sum[i] + dq
            top, bottom = total[:HALF], total[HALF:]
            own_half[i] = jnp.where(c == 0, top, bottom)
            sent_half[i] = jnp.where(c == 0, bottom, top)
            swap_half(i).start()

        @pl.when(ended)
        def _():
            combine(before)

        return 0

    lax.fori_loop(0, 2 * n_z, compute, 0)
    send_keys(0)
    combine(n_z - 2)
    combine(n_z - 1)

    pltpu.make_async_copy(dq_in.at[pl.ds(1, n_z - 1)], dq_in.at[pl.ds(1, n_z - 1)], dq_recv).wait()
    total = own_half[0]
    for i in range(1, n_z):
        total = total + dq_in[i].astype(F32)
    dq_done[...] = total.astype(BF16)
    out_query.start()

    def settle(buf, n, sem):
        pltpu.make_async_copy(buf.at[pl.ds(0, n)], buf.at[pl.ds(0, n)], sem).wait()

    @pl.when(to_self)
    def _():
        settle(op_ref, n_h - 1, p_recv)
        own_tile.wait()

    @pl.when(jnp.logical_not(to_self))
    def _():
        settle(op_ref, n_h, p_recv)

    out_query.wait()

    for way in (0, 1):
        near(way).wait_send()
        fourth(way).wait_send()
        for half in (0, 1):
            far(way, half).wait_send()
            third(way, half).wait_send()
    for i in range(n_z):
        pair(i).wait_send()
        swap_half(i).wait_send()
    settle(dq_out, n_z - 1, dq_send)
    settle(stored, n_z - 1, stat_send)

    @pl.when(to_self)
    def _():
        settle(p_out, slots * n_z - 1, p_send)

    @pl.when(jnp.logical_not(to_self))
    def _():
        settle(p_out, slots * n_z, p_send)

    for place in range(slots):
        left = pltpu.make_async_copy(kvb.at[place], kvb.at[place], kv_send.at[place])
        unless_self(place, left.wait)


def last_kernel(q_ref, p_ref, oq_ref, ok_ref, ov_ref, wide):
    n_h, both, _ = p_ref.shape
    dr = both // 2
    oq_ref[...] = q_ref[...]
    wide[...] = p_ref[...].astype(F32).reshape(n_h * both, LANES)
    for which, ref in enumerate((ok_ref, ov_ref)):
        picked = [wide[pl.ds(which * dr + d, n_h, stride=both), :] for d in range(dr)]
        ref[...] = jnp.concatenate(picked, 0).T.astype(BF16)


def on_device(kv_states, queries_t, grad_out_t, log_norm, delta, lengths):
    n_z, n_s = lax.axis_size("grp"), lax.axis_size("seq")
    n_h = n_s // 2
    rows, cols = kv_states.shape
    tokens = queries_t.shape[1]
    slots = n_h // n_z
    keys = slots * rows
    dr = DH // n_z
    given = (kv_states, queries_t, grad_out_t, log_norm, delta, lengths)
    hbm = pl.BlockSpec(memory_space=pl.ANY)
    vmem = pl.BlockSpec(memory_space=pltpu.VMEM)
    dma = pltpu.SemaphoreType.DMA
    grad_query, tiles = pl.pallas_call(
        functools.partial(kernel, n_z, n_h, rows * n_s),
        out_shape=(
            jax.ShapeDtypeStruct((HALF, tokens), BF16),
            jax.ShapeDtypeStruct((n_h, 2 * dr, LANES), BF16),
        ),
        in_specs=[hbm] * 6,
        out_specs=(hbm,) * 2,
        scratch_shapes=[
            pltpu.VMEM((rows, cols), BF16),
            pltpu.VMEM((n_h, tokens), F32),
            pltpu.VMEM((n_h, tokens), F32),
            pltpu.SMEM(lengths.shape, jnp.int32),
            pltpu.VMEM((n_z, 2 * tokens // LANES, LANES), F32),
            pltpu.VMEM((n_z, STATS, tokens), BF16),
            pltpu.VMEM((slots, rows, LANES), BF16),
            pltpu.VMEM((slots, rows, LANES), BF16),
            pltpu.VMEM((n_z, 2, PART, tokens), BF16),
            pltpu.VMEM((2, keys, DEPTH), BF16),
            pltpu.VMEM((2, DH, keys // 2), BF16),
            pltpu.VMEM((keys, 2 * DH), F32),
            pltpu.VMEM((n_z, DH, tokens), F32),
            pltpu.VMEM((n_z, HALF, tokens), F32),
            pltpu.VMEM((n_z, HALF, tokens), F32),
            pltpu.VMEM((n_z, HALF, tokens), F32),
            pltpu.VMEM((n_z, HALF, tokens), BF16),
            pltpu.VMEM((n_z, HALF, tokens), BF16),
            pltpu.VMEM((slots * n_z, 2 * dr, LANES), BF16),
            pltpu.VMEM((HALF, tokens), BF16),
            dma((6,)), dma((2,)),
            dma, dma,
            dma((slots,)), dma((slots,)),
            dma((2,)), dma((2,)),
            dma((2, 2)), dma((2, 2)),
            dma((2, 2)), dma((2, 2)),
            dma((2,)), dma((2,)),
            dma((n_z,)), dma((n_z,)),
            dma((n_z,)), dma((n_z,)),
            dma, dma, dma, dma,
        ],
        compiler_params=pltpu.CompilerParams(
            collective_id=0, has_side_effects=True, vmem_limit_bytes=63 * 1024 * 1024
        ),
        cost_estimate=pl.CostEstimate(
            flops=10 * DH * keys * tokens * n_z,
            bytes_accessed=4 * 1024 * 1024,
            transcendentals=keys * tokens * n_z,
        ),
    )(*given)
    return pl.pallas_call(
        last_kernel,
        out_shape=(
            jax.ShapeDtypeStruct((HALF, tokens), BF16),
            jax.ShapeDtypeStruct((rows, dr * n_h), BF16),
            jax.ShapeDtypeStruct((rows, dr * n_h), BF16),
        ),
        in_specs=[vmem] * 2,
        out_specs=(vmem,) * 3,
        scratch_shapes=[pltpu.VMEM((n_h * 2 * dr, LANES), F32)],
    )(grad_query, tiles)


def solution(mesh):
    placed = (
        P("seq", None),
        P("seq", "grp"),
        P("seq", "grp"),
        P(None, "grp"),
        P(None, "grp"),
        P("grp"),
    )
    return jax.shard_map(
        on_device,
        mesh=mesh,
        in_specs=placed,
        out_specs=(P("seq", "grp"), P("seq", "grp"), P("seq", "grp")),
        check_vma=False,
    )
```

```python
import functools
import math

import jax
import jax.numpy as jnp
from jax import lax
from jax.experimental import pallas as pl
from jax.experimental.pallas import tpu as pltpu
from jax.sharding import PartitionSpec as P

DH = 64
LEN = 256
HALF = DH // 2
STATS = 16
PART = 2 * HALF
DEPTH = 2 * PART + STATS
LANES = 128
MESH = pl.DeviceIdType.MESH
F32 = jnp.float32
BF16 = jnp.bfloat16

AWAY = (
    ((4, 3), (3, 2), (5, 2), (4, 2)),
    ((3, 3), (5, 1), (6, 2), (4, 1)),
    ((3, 1), (5, 3), (2, 2), (4, 0)),
    ((2, 3), (6, 1), (7, 2), (5, 0)),
    ((2, 1), (6, 3), (1, 2), (3, 0)),
    ((1, 1), (1, 3), (7, 1), (7, 3)),
    ((7, 0), (0, 2), (2, 0), (6, 0)),
    ((0, 0), (0, 1), (0, 3), (1, 0)),
)

NT = (((1,), (1,)), ((), ()))
NN = (((1,), (0,)), ((), ()))


def dot(a, b, dims=NN):
    return lax.dot_general(a, b, dims, preferred_element_type=F32)


def exchange_lanes(tiles, unit):
    count = len(tiles)
    lane = lax.broadcasted_iota(jnp.int32, tiles[0].shape, 1)
    step = 1
    while step < count:
        shift = step * unit
        low = (lane & shift) == 0
        made = list(tiles)
        for a in range(count):
            if a & step == 0:
                x, y = tiles[a], tiles[a | step]
                made[a] = jnp.where(low, x, pltpu.roll(y, shift, 1))
                made[a | step] = jnp.where(low, pltpu.roll(x, LANES - shift, 1), y)
        tiles = made
        step *= 2
    return tiles


def kernel(
    n_z, n_h, keys_all,
    kv_hbm, q_hbm, g_hbm, ln_hbm, dl_hbm, len_hbm,
    oq_ref, op_ref,
    kvx, lnv, dlv, len_ref, stored, stats, kvs, kvb, blocks, lhs, keys_t, acc,
    dq_sum, own_half, sent_half, got_half, dq_out, dq_in, p_out, dq_done,
    in_sem, out_sem, stat_send, stat_recv, kv_send, kv_recv, near_send, near_recv, far_send, far_recv,
    third_send, third_recv, fourth_send, fourth_recv, pair_send, pair_recv,
    half_send, half_recv, dq_send, dq_recv, p_send, p_recv,
):
    z = lax.axis_index("grp")
    s = lax.axis_index("seq")
    h = s // 2
    c = s - 2 * h
    partner = 2 * h + 1 - c
    rows = kvx.shape[0]
    tokens = blocks.shape[3]
    span = tokens // 2
    slots = kvb.shape[0]
    chunk = slots * rows // 2
    dr = DH // n_z

    width = n_z // 2
    runs = n_h // width
    run = h // width
    along_run = h - run * width
    to_self = z == n_z - 1

    def choose(table, i):
        out = jnp.int32(table[-1])
        for k in range(len(table) - 1):
            out = jnp.where(i == k, table[k], out)
        return out

    sources, served = [], []
    for place in range(slots):
        down = choose([AWAY[k][place][0] for k in range(n_z)], z)
        right = choose([AWAY[k][place][1] for k in range(n_z)], z)
        sources.append(lax.rem(run + down, runs) * width + lax.rem(along_run + right, width))
        served.append(
            lax.rem(run + runs - down, runs) * width + lax.rem(along_run + width - right, width)
        )

    def unless_self(place, go):
        if place == 0:
            pl.when(jnp.logical_not(to_self))(go)
        else:
            go()

    barrier = pltpu.get_barrier_semaphore()

    def greet(device):
        pl.semaphore_signal(barrier, inc=1, device_id=device, device_id_type=MESH)

    def greet_line(i, _):
        greet((lax.rem(z + i, n_z), s))
        return 0

    for place in range(slots):
        unless_self(place, functools.partial(greet, (z, 2 * sources[place] + c)))
    lax.fori_loop(1, n_z, greet_line, 0)
    greet((z, partner))

    loads = [
        pltpu.make_async_copy(ln_hbm, lnv, in_sem.at[0]),
        pltpu.make_async_copy(dl_hbm, dlv, in_sem.at[1]),
        pltpu.make_async_copy(q_hbm, blocks.at[z, c, pl.ds(0, HALF)], in_sem.at[2]),
        pltpu.make_async_copy(g_hbm, blocks.at[z, c, pl.ds(HALF, HALF)], in_sem.at[3]),
    ]
    for load in loads:
        load.start()
    load_lengths = pltpu.make_async_copy(len_hbm, len_ref, in_sem.at[5])
    load_lengths.start()
    load_kv = pltpu.make_async_copy(kv_hbm, kvx, in_sem.at[4])

    load_kv.start()

    loads[0].wait()
    loads[1].wait()
    load_lengths.wait()
    place = lax.broadcasted_iota(jnp.int32, (1, tokens), 1)
    limit = jnp.zeros((1, tokens), jnp.int32)
    for a in range(tokens // LEN):
        limit = jnp.where(place // LEN == a, len_ref[a], limit)
    norm = -(lnv[pl.ds(h, 1), :] + math.log(keys_all))
    norm = jnp.where(lax.rem(place, LEN) < limit, norm, -1e30)
    less = -dlv[pl.ds(h, 1), :]
    for k in range(tokens // LANES):
        columns = slice(k * LANES, (k + 1) * LANES)
        stored[z, k : k + 1] = norm[:, columns]
        stored[z, tokens // LANES + k : tokens // LANES + k + 1] = less[:, columns]
    loads[2].wait()
    loads[3].wait()

    load_kv.wait()

    group = LANES // slots
    at = lax.broadcasted_iota(jnp.int32, (2 * LANES, LANES), 0)
    to = lax.broadcasted_iota(jnp.int32, (2 * LANES, LANES), 1)
    wanted = jnp.zeros_like(to)
    for place in range(slots):
        wanted = jnp.where(to // group == place, served[place], wanted)
    by_head = lax.rem(at, n_h) == wanted
    per = 2 * LANES // n_h
    picked = jnp.zeros((slots * rows, LANES), F32)
    for step in range(group // per):
        one_hot = by_head & (lax.rem(to, group) == step * per + at // n_h)
        taken = [
            kvx[:, (m * group // per + step) * 2 * LANES : (m * group // per + step + 1) * 2 * LANES]
            for m in range(slots)
        ]
        picked += dot(jnp.concatenate(taken, 0), jnp.where(one_hot, 1.0, 0.0).astype(BF16))
    tiles = exchange_lanes([picked[m * rows : (m + 1) * rows] for m in range(slots)], group)
    for place in range(slots):
        kvs[place] = tiles[place].astype(BF16)

    @pl.when(to_self)
    def _():
        kvb[0] = kvs[0]

    pl.semaphore_wait(barrier, n_z + slots - jnp.where(to_self, 1, 0))

    every = pl.ds(0, tokens)

    def columns_of(half):
        return pl.ds(pl.multiple_of(half * span, span), span)


    def order(i):
        t = (i + 1) // 2
        return lax.rem(jnp.where(lax.rem(i, 2) == 1, z - t, z + t) + n_z, n_z)

    def along(way, hops, block, columns, send, recv):
        to = lax.rem(z + jnp.where(way == 0, hops, n_z - hops), n_z)
        ref = blocks.at[block, c, :, columns]
        return pltpu.make_async_remote_copy(
            src_ref=ref, dst_ref=ref, send_sem=send, recv_sem=recv,
            device_id=(to, s), device_id_type=MESH,
        )

    def near(way):
        return along(way, 1, z, every, near_send.at[way], near_recv.at[way])

    def far(way, half):
        return along(way, 2, z, columns_of(half), far_send.at[way, half], far_recv.at[way, half])

    def third(way, half):
        block = order(3 + way)
        return along(way, 1, block, columns_of(half), third_send.at[way, half], third_recv.at[way, half])

    def fourth(way):
        return along(way, 2, order(3 + way), columns_of(way), fourth_send.at[way], fourth_recv.at[way])

    def pair(i):
        ref = blocks.at[order(i), c]
        return pltpu.make_async_remote_copy(
            src_ref=ref, dst_ref=ref,
            send_sem=pair_send.at[i], recv_sem=pair_recv.at[i],
            device_id=(z, partner), device_id_type=MESH,
        )

    for half in (0, 1):
        for way in (0, 1):
            far(way, half).start()

    pair(0).start()

    for place in reversed(range(slots)):
        copy = pltpu.make_async_remote_copy(
            src_ref=kvs.at[place], dst_ref=kvb.at[place],
            send_sem=kv_send.at[place], recv_sem=kv_recv.at[place],
            device_id=(z, 2 * served[place] + c), device_id_type=MESH,
        )
        unless_self(place, copy.start)

    def send_stored(i, _):
        pltpu.make_async_remote_copy(
            src_ref=stored.at[z], dst_ref=stored.at[z], send_sem=stat_send, recv_sem=stat_recv,
            device_id=(lax.rem(z + i, n_z), s), device_id_type=MESH,
        ).start()
        return 0

    for way in (0, 1):
        near(way).start()
    lax.fori_loop(1, n_z, send_stored, 0)
    lane = lax.broadcasted_iota(jnp.int32, (LANES, DEPTH), 0)
    col = lax.broadcasted_iota(jnp.int32, (LANES, DEPTH), 1)
    side = col // PART
    within = col - side * PART
    is_key = (side < 2) & (within < HALF)
    is_value = (side < 2) & (within >= HALF)
    for_scores = jnp.where(is_key & (lane == side * HALF + within), 1.0, 0.0).astype(BF16)
    for_dprobs = jnp.where(
        is_value & (lane == DH + side * HALF + within - HALF), 1.0, 0.0
    ).astype(BF16)
    one = lax.broadcasted_iota(jnp.int32, (1, DEPTH), 1) - 2 * PART
    ones_s = jnp.where((one >= 0) & (one < 3), 1.0, 0.0)
    ones_p = jnp.where((one >= 3) & (one < 6), 1.0, 0.0)
    lane_t = lax.broadcasted_iota(jnp.int32, (DH, LANES), 1)
    row_t = lax.broadcasted_iota(jnp.int32, (DH, LANES), 0)
    for_keys = jnp.where(lane_t == row_t, 1.0, 0.0).astype(BF16)
    acc[...] = jnp.zeros_like(acc)

    first_way = jnp.where((z >= n_z // 4) & (z < 3 * n_z // 4), 0, 1)
    for half in (0, 1):
        for way in (first_way, 1 - first_way):
            far(way, half).wait_recv()
            third(way, half).start()

            @pl.when(way == half)
            def _():
                fourth(way).start()

    for way in (0, 1):
        pair(3 + way).start()
    for way in (0, 1):
        near(way).wait_recv()
        pair(1 + way).start()

    pltpu.make_async_copy(stored.at[pl.ds(1, n_z - 1)], stored.at[pl.ds(1, n_z - 1)], stat_recv).wait()
    at = lax.broadcasted_iota(jnp.int32, (STATS, tokens), 0)

    def split(b, _):
        rows_of = tokens // LANES
        norm = jnp.concatenate([stored[b, k : k + 1] for k in range(rows_of)], 1)
        less = jnp.concatenate([stored[b, rows_of + k : rows_of + k + 1] for k in range(rows_of)], 1)
        both = jnp.where(at < 3, norm, less)
        high = both.astype(BF16).astype(F32)
        middle = (both - high).astype(BF16).astype(F32)
        low = both - high - middle
        which = lax.rem(at, 3)
        out = jnp.where(which == 0, high, jnp.where(which == 1, middle, low))
        stats[b] = jnp.where(at < 6, out, 0.0).astype(BF16)
        return 0

    lax.fori_loop(0, n_z, split, 0)

    def keys_in(part):
        for place in (part * slots // 2, part * slots // 2 + 1):

            arrived = pltpu.make_async_copy(kvb.at[place], kvb.at[place], kv_recv.at[place])
            unless_self(place, arrived.wait)

        at = pl.ds(part * chunk, chunk)
        mixed = kvb[pl.ds(part * slots // 2, slots // 2)].reshape(chunk, LANES)
        lhs[0, at] = (dot(mixed, for_scores) + ones_s).astype(BF16)
        lhs[1, at] = (dot(mixed, for_dprobs) + ones_p).astype(BF16)
        keys_t[part] = dot(for_keys, mixed, NT).astype(BF16)

    keys_in(0)

    def swap_half(i):
        return pltpu.make_async_remote_copy(
            src_ref=sent_half.at[i], dst_ref=got_half.at[i],
            send_sem=half_send.at[i], recv_sem=half_recv.at[i],
            device_id=(z, partner), device_id_type=MESH,
        )

    def dq_copy(i):
        return pltpu.make_async_remote_copy(
            src_ref=dq_out.at[i], dst_ref=dq_in.at[i], send_sem=dq_send, recv_sem=dq_recv,
            device_id=(order(i), s), device_id_type=MESH,
        )

    def combine(i):
        swap_half(i).wait_recv()
        total = own_half[i] + got_half[i]
        own_half[i] = total
        dq_out[i] = total.astype(BF16)

        @pl.when(i > 0)
        def _():
            dq_copy(i).start()

    own_tile = pltpu.make_async_copy(p_out.at[z], op_ref.at[h], out_sem.at[0])
    out_query = pltpu.make_async_copy(dq_done, oq_ref, out_sem.at[1])

    def send_keys(part):
        turned = acc[part * chunk : (part + 1) * chunk].T.reshape(2, n_z, dr, chunk)
        first = part * slots // 2
        for place in range(slots // 2):
            columns = slice(place * rows, (place + 1) * rows)
            for g in range(n_z):
                tile = jnp.concatenate([turned[0, g, :, columns], turned[1, g, :, columns]], 0)
                p_out[(first + place) * n_z + g] = tile.astype(BF16)
        if part == 0:
            pl.when(to_self)(own_tile.start)

        for place in reversed(range(first, first + slots // 2)):

            def send(g, _):
                def go():
                    pltpu.make_async_remote_copy(
                        src_ref=p_out.at[place * n_z + g], dst_ref=op_ref.at[h],
                        send_sem=p_send, recv_sem=p_recv,
                        device_id=(g, 2 * sources[place] + c), device_id_type=MESH,
                    ).start()

                if place == 0:
                    pl.when(jnp.logical_not(to_self & (g == z)))(go)
                else:
                    go()
                return 0

            lax.fori_loop(0, n_z, send, 0)

    early = 5

    def step_of(j):
        i = jnp.where(j < early, j, jnp.where(j < early + n_z, j - early, j - n_z))
        return i, ((j >= early) & (j < 2 * early)) | (j >= n_z + early)

    keys_at, third_at, fourth_at, far_done = 0, 5, 7, 13

    def compute(j, _):
        part = jnp.where((j >= early) & (j < early + n_z), 1, 0)
        i, ends = step_of(j)
        opens = jnp.logical_not(ends)
        before, ended = step_of(j - 2)

        @pl.when(j == keys_at)
        def _():
            keys_in(1)

        @pl.when(j == third_at)
        def _():
            for way in (0, 1):
                for half in (0, 1):
                    third(way, half).wait_recv()
                pair(5 + way).start()

        @pl.when(j == fourth_at)
        def _():
            for way in (0, 1):
                fourth(way).wait_recv()
            pair(7).start()

        @pl.when(j == far_done)
        def _():
            send_keys(1)

        block = order(i)

        @pl.when(opens)
        def _():
            pltpu.make_async_copy(
                blocks.at[block, 1 - c], blocks.at[block, 1 - c], pair_recv.at[i]
            ).wait()

        rhs = jnp.concatenate([blocks[block].reshape(2 * PART, tokens), stats[block]], 0)
        blank = jnp.zeros((DH, tokens), BF16)
        q_rows = jnp.concatenate([rhs[:HALF], rhs[PART : PART + HALF], blank], 0)
        g_rows = jnp.concatenate([blank, rhs[HALF:PART], rhs[PART + HALF : 2 * PART]], 0)
        at = pl.ds(pl.multiple_of(part * chunk, chunk), chunk)
        both = dot(lhs[:, at].reshape(2 * chunk, DEPTH), rhs)
        probs = jnp.exp(both[:chunk])
        dscores = probs * both[chunk:]
        probs = probs.astype(BF16)
        dscores = dscores.astype(BF16)
        acc[at] += dot(dscores, q_rows, NT) + dot(probs, g_rows, NT)
        dq = dot(keys_t[part], dscores)

        @pl.when(opens)
        def _():
            dq_sum[i] = dq

        @pl.when(jnp.logical_not(opens))
        def _():
            total = dq_sum[i] + dq
            top, bottom = total[:HALF], total[HALF:]
            own_half[i] = jnp.where(c == 0, top, bottom)
            sent_half[i] = jnp.where(c == 0, bottom, top)
            swap_half(i).start()

        @pl.when(ended)
        def _():
            combine(before)

        return 0

    lax.fori_loop(0, 2 * n_z, compute, 0)
    send_keys(0)
    combine(n_z - 2)
    combine(n_z - 1)

    pltpu.make_async_copy(dq_in.at[pl.ds(1, n_z - 1)], dq_in.at[pl.ds(1, n_z - 1)], dq_recv).wait()
    total = own_half[0]
    for i in range(1, n_z):
        total = total + dq_in[i].astype(F32)
    dq_done[...] = total.astype(BF16)
    out_query.start()

    def settle(buf, n, sem):
        pltpu.make_async_copy(buf.at[pl.ds(0, n)], buf.at[pl.ds(0, n)], sem).wait()

    @pl.when(to_self)
    def _():
        settle(op_ref, n_h - 1, p_recv)
        own_tile.wait()

    @pl.when(jnp.logical_not(to_self))
    def _():
        settle(op_ref, n_h, p_recv)

    out_query.wait()

    for way in (0, 1):
        near(way).wait_send()
        fourth(way).wait_send()
        for half in (0, 1):
            far(way, half).wait_send()
            third(way, half).wait_send()
    for i in range(n_z):
        pair(i).wait_send()
        swap_half(i).wait_send()
    settle(dq_out, n_z - 1, dq_send)
    settle(stored, n_z - 1, stat_send)

    @pl.when(to_self)
    def _():
        settle(p_out, slots * n_z - 1, p_send)

    @pl.when(jnp.logical_not(to_self))
    def _():
        settle(p_out, slots * n_z, p_send)

    for place in range(slots):
        left = pltpu.make_async_copy(kvb.at[place], kvb.at[place], kv_send.at[place])
        unless_self(place, left.wait)


def last_kernel(q_ref, p_ref, oq_ref, ok_ref, ov_ref, wide):
    n_h, both, _ = p_ref.shape
    dr = both // 2
    oq_ref[...] = q_ref[...]
    wide[...] = p_ref[...].astype(F32).reshape(n_h * both, LANES)
    for which, ref in enumerate((ok_ref, ov_ref)):
        picked = [wide[pl.ds(which * dr + d, n_h, stride=both), :] for d in range(dr)]
        ref[...] = jnp.concatenate(picked, 0).T.astype(BF16)


def on_device(kv_states, queries_t, grad_out_t, log_norm, delta, lengths):
    n_z, n_s = lax.axis_size("grp"), lax.axis_size("seq")
    n_h = n_s // 2
    rows, cols = kv_states.shape
    tokens = queries_t.shape[1]
    slots = n_h // n_z
    keys = slots * rows
    dr = DH // n_z
    given = (kv_states, queries_t, grad_out_t, log_norm, delta, lengths)
    hbm = pl.BlockSpec(memory_space=pl.ANY)
    vmem = pl.BlockSpec(memory_space=pltpu.VMEM)
    dma = pltpu.SemaphoreType.DMA
    grad_query, tiles = pl.pallas_call(
        functools.partial(kernel, n_z, n_h, rows * n_s),
        out_shape=(
            jax.ShapeDtypeStruct((HALF, tokens), BF16),
            jax.ShapeDtypeStruct((n_h, 2 * dr, LANES), BF16),
        ),
        in_specs=[hbm] * 6,
        out_specs=(hbm,) * 2,
        scratch_shapes=[
            pltpu.VMEM((rows, cols), BF16),
            pltpu.VMEM((n_h, tokens), F32),
            pltpu.VMEM((n_h, tokens), F32),
            pltpu.SMEM(lengths.shape, jnp.int32),
            pltpu.VMEM((n_z, 2 * tokens // LANES, LANES), F32),
            pltpu.VMEM((n_z, STATS, tokens), BF16),
            pltpu.VMEM((slots, rows, LANES), BF16),
            pltpu.VMEM((slots, rows, LANES), BF16),
            pltpu.VMEM((n_z, 2, PART, tokens), BF16),
            pltpu.VMEM((2, keys, DEPTH), BF16),
            pltpu.VMEM((2, DH, keys // 2), BF16),
            pltpu.VMEM((keys, 2 * DH), F32),
            pltpu.VMEM((n_z, DH, tokens), F32),
            pltpu.VMEM((n_z, HALF, tokens), F32),
            pltpu.VMEM((n_z, HALF, tokens), F32),
            pltpu.VMEM((n_z, HALF, tokens), F32),
            pltpu.VMEM((n_z, HALF, tokens), BF16),
            pltpu.VMEM((n_z, HALF, tokens), BF16),
            pltpu.VMEM((slots * n_z, 2 * dr, LANES), BF16),
            pltpu.VMEM((HALF, tokens), BF16),
            dma((6,)), dma((2,)),
            dma, dma,
            dma((slots,)), dma((slots,)),
            dma((2,)), dma((2,)),
            dma((2, 2)), dma((2, 2)),
            dma((2, 2)), dma((2, 2)),
            dma((2,)), dma((2,)),
            dma((n_z,)), dma((n_z,)),
            dma((n_z,)), dma((n_z,)),
            dma, dma, dma, dma,
        ],
        compiler_params=pltpu.CompilerParams(
            collective_id=0, has_side_effects=True, vmem_limit_bytes=63 * 1024 * 1024
        ),
        cost_estimate=pl.CostEstimate(
            flops=10 * DH * keys * tokens * n_z,
            bytes_accessed=4 * 1024 * 1024,
            transcendentals=keys * tokens * n_z,
        ),
    )(*given)
    return pl.pallas_call(
        last_kernel,
        out_shape=(
            jax.ShapeDtypeStruct((HALF, tokens), BF16),
            jax.ShapeDtypeStruct((rows, dr * n_h), BF16),
            jax.ShapeDtypeStruct((rows, dr * n_h), BF16),
        ),
        in_specs=[vmem] * 2,
        out_specs=(vmem,) * 3,
        scratch_shapes=[pltpu.VMEM((n_h * 2 * dr, LANES), F32)],
    )(grad_query, tiles)


def solution(mesh):
    placed = (
        P("seq", None),
        P("seq", "grp"),
        P("seq", "grp"),
        P(None, "grp"),
        P(None, "grp"),
        P("grp"),
    )
    return jax.shard_map(
        on_device,
        mesh=mesh,
        in_specs=placed,
        out_specs=(P("seq", "grp"), P("seq", "grp"), P("seq", "grp")),
        check_vma=False,
    )
```
